32 devices in a mesh: atom: 8 (over z, x), chan: 2 (over core), rep: 2 (over y).
Axes of the slice: x: 2, y: 2, z: 4, core: 2. Of those that a mesh axis runs over, the one named last changes fastest.
Arguments:
- feats: bfloat16 [2, 128, 81, 128], P('rep', 'chan', None, 'atom'), may hold values from -6 to 6
- neighbors: int32 [2, 128, 32], P('rep', 'atom'), may hold values from 0 to 127, as said below
- counts: int32 [2, 128], P('rep', 'atom'), may hold values from 1 to 32, as said below
- radial: bfloat16 [2, 8, 4096], P('rep', None, 'atom'), may hold values from 2 to 6
- filter_weight: bfloat16 [8, 128, 81], P(None, 'chan'), may hold values from -0.3125 to 0.3125
- message_grad: bfloat16 [2, 128, 81, 4096], P('rep', 'chan', None, 'atom'), may hold values from -2 to 2
Outputs:
- feat_grad: float32 [2, 128, 81, 128], P('rep', 'chan', None, 'atom')
- radial_grad: float32 [2, 8, 4096], P('rep', None, 'atom')
- weight_grad: float32 [8, 128, 81], P(None, 'chan')
The draws below stay inside these ranges and needn't reach their ends.
Inputs may be any that keep to these rules, and one draw needn't show every extreme that they name: `neighbors`: each source atom lies, counted cyclically, in the block of 16 consecutive atoms that holds its receiver or in one of the 2 such blocks on either side. `counts`: some atom of every crystal has all 32 slots valid.
All inputs are finite; a program needn't handle non-finite values.
Results may differ from the reference program's by a relative error of at most 0.0054.
Values may be sent and summed in bfloat16 or wider, within the bound.
A program may use at most 64 MiB of HBM per device.

```python
import jax
import jax.numpy as jnp
from jax import lax

C = 128
BASIS = 9
POINTS = 16
K = 8
SLOTS = 32
REACH = 2
ATOM_DEV = 16
G = 81
SAMPLES = 256
ATOMS = 128
EDGES = 4096
BATCH = 2


def draw_neighbors(key, part):
    first_key, second_key = jax.random.split(jax.random.fold_in(key, 11))
    shape = (BATCH, ATOMS, SLOTS)
    offsets = jax.random.randint(first_key, shape, -REACH, REACH + 1)
    inside = jax.random.randint(second_key, shape, 0, ATOM_DEV)
    block_count = ATOMS // ATOM_DEV
    blocks = (jnp.arange(ATOMS, dtype=jnp.int32) // ATOM_DEV)[None, :, None]
    return ((blocks + offsets) % block_count * ATOM_DEV + inside).astype(jnp.int32)


def draw_counts(key, part):
    first_key, second_key, third_key = jax.random.split(jax.random.fold_in(key, 23), 3)
    block_count = ATOMS // ATOM_DEV
    base = jax.random.randint(first_key, (BATCH, block_count), 4, SLOTS + 1)
    jitter = jax.random.randint(second_key, (BATCH, ATOMS), -3, 4)
    counted = jnp.clip(jnp.repeat(base, ATOM_DEV, axis=1) + jitter, 1, SLOTS)
    chosen = jax.random.randint(third_key, (BATCH, 1), 0, ATOMS)
    counted = jnp.where(jnp.arange(ATOMS, dtype=jnp.int32)[None, :] == chosen, SLOTS, counted)
    return counted.astype(jnp.int32)


def block_levels(rng, dims, cuts, smallest, top_value):
    loudness = 1.0
    for position, blocks in cuts:
        steps = jax.random.uniform(jax.random.fold_in(jax.random.fold_in(rng, 6), position), (blocks,), jnp.float32, smallest / len(cuts), top_value / len(cuts))
        loudness = loudness * jnp.repeat(jnp.exp(steps), dims[position] // blocks).reshape((-1,) + (1,) * (len(dims) - 1 - position))
    return loudness


def scatter_about(own_key, dims, spread, most, cuts=(), kind=jnp.bfloat16):
    factor_of = block_levels(own_key, dims, cuts, -0.22, 0.18) if cuts else 1.0
    values = jax.random.normal(own_key, dims, jnp.float32) * spread * factor_of
    return jnp.minimum(jnp.maximum(values, -most), most).astype(kind)


def setup_inputs(seed: int = 0) -> dict:
    arg_keys = jax.random.split(jax.random.key(seed), 7)
    feats = scatter_about(arg_keys[0], (BATCH, C, G, ATOMS), 1.0, 6.0, ((0, 2), (1, 2), (3, 8)))
    neighbors = draw_neighbors(jax.random.fold_in(arg_keys[6], 71), 0)
    counts = draw_counts(jax.random.fold_in(arg_keys[6], 71), 0)
    radial = jnp.clip(2.0 + 4.0 * jax.random.uniform(arg_keys[3], (BATCH, K, EDGES), jnp.float32) ** block_levels(arg_keys[3], (BATCH, K, EDGES), ((0, 2), (2, 8)), -0.2, 0.2), 2.0, 6.0).astype(jnp.bfloat16)
    filter_weight = scatter_about(arg_keys[4], (K, C, G), 0.02, 0.3125, ((1, 2),))
    message_grad = scatter_about(arg_keys[5], (BATCH, C, G, EDGES), 0.15, 2.0, ((0, 2), (1, 2), (3, 8)))
    return {"feats": feats, "neighbors": neighbors, "counts": counts, "radial": radial, "filter_weight": filter_weight, "message_grad": message_grad}


def basis_table():
    points = jnp.arange(POINTS, dtype=jnp.float32) * jnp.float32(2.0 * 3.141592653589793 / POINTS)
    degree_index = jnp.arange(BASIS, dtype=jnp.int32)
    frequency = ((degree_index + 1) // 2).astype(jnp.float32)
    angles = frequency[:, None] * points[None, :]
    root_two = jnp.sqrt(jnp.float32(2.0))
    single = jnp.where(degree_index[:, None] == 0, jnp.ones_like(angles), jnp.where(degree_index[:, None] % 2 == 1, root_two * jnp.cos(angles), root_two * jnp.sin(angles)))
    product = single[:, None, :, None] * single[None, :, None, :]
    return product.reshape(G, SAMPLES).astype(jnp.bfloat16)

def channel_terms(gathered, grad_c, weight_c, radial_e, valid_mask, synth_table, synth_rows):
    filter_edge = jnp.dot(weight_c.T, radial_e, preferred_element_type=jnp.float32).astype(jnp.bfloat16)
    feat_grid = jnp.dot(synth_rows, gathered, preferred_element_type=jnp.float32)
    filt_grid = jnp.dot(synth_rows, filter_edge, preferred_element_type=jnp.float32)
    weighted = jnp.dot(synth_rows, grad_c, preferred_element_type=jnp.float32) * (valid_mask / SAMPLES)[None, :]
    feat_side = (weighted * filt_grid).astype(jnp.bfloat16)
    filt_side = (weighted * feat_grid).astype(jnp.bfloat16)
    edge_grad = jnp.dot(synth_table, feat_side, preferred_element_type=jnp.float32).astype(jnp.bfloat16)
    filt_grad = jnp.dot(synth_table, filt_side, preferred_element_type=jnp.float32).astype(jnp.bfloat16)
    radial_part = jnp.dot(weight_c, filt_grad, preferred_element_type=jnp.float32)
    weight_part = jnp.dot(radial_e, filt_grad.T, preferred_element_type=jnp.float32)
    return (edge_grad, radial_part, weight_part)

def reference(feats, neighbors, counts, radial, filter_weight, message_grad):
    synth_table = basis_table()
    synth_rows = synth_table.T
    feat_list = []
    radial_list = []
    weight_total = jnp.zeros((C, K, G), jnp.float32)
    for batch_row in range(BATCH):
        sources = neighbors[batch_row].reshape(-1).astype(jnp.int32)
        valid_mask = (jnp.arange(SLOTS, dtype=jnp.int32)[None, :] < counts[batch_row][:, None]).reshape(-1).astype(jnp.float32)
        radial_e = radial[batch_row]

        def per_channel(channel):
            gathered = jnp.take(feats[batch_row, channel], sources, axis=1)
            weight_c = filter_weight[:, channel, :]
            edge_grad, radial_part, weight_part = channel_terms(gathered, message_grad[batch_row, channel], weight_c, radial_e, valid_mask, synth_table, synth_rows)
            source_grad = jax.ops.segment_sum(edge_grad.astype(jnp.float32).T, sources, num_segments=ATOMS).T
            return (source_grad, radial_part, weight_part)
        source_grad, radial_part, weight_part = lax.map(per_channel, jnp.arange(C, dtype=jnp.int32))
        feat_list.append(source_grad)
        radial_list.append(lax.optimization_barrier(jnp.sum(radial_part, axis=0)))
        weight_total = weight_total + weight_part
    weight_grad = jnp.transpose(weight_total, (1, 0, 2)) / (ATOMS * BATCH)
    return (jnp.stack(feat_list), jnp.stack(radial_list), weight_grad)
```

```python
import functools

import jax
import jax.numpy as jnp
import numpy as np
from jax import lax
from jax.experimental import pallas as pl
from jax.experimental.pallas import tpu as pltpu
from jax.sharding import PartitionSpec as P

BASIS = 9
POINTS = 13
SAMPLES = POINTS * POINTS
SAMPLES_PAD = -(-SAMPLES // 16) * 16
SLOTS = 32
REACH = 2
G = 81
G_PAD = 96
GROUP = 4


def basis_table():
    points = np.arange(POINTS) * (2.0 * np.pi / POINTS)
    degree_index = np.arange(BASIS)
    angles = ((degree_index + 1) // 2)[:, None] * points[None, :]
    single = np.where(
        degree_index[:, None] == 0,
        1.0,
        np.sqrt(2.0) * np.where(degree_index[:, None] % 2 == 1, np.cos(angles), np.sin(angles)),
    )
    product = (single[:, None, :, None] * single[None, :, None, :]).reshape(G, SAMPLES)
    padded = np.zeros((G_PAD, SAMPLES_PAD), np.float32)
    padded[:G, :SAMPLES] = product
    return padded


def passed_along(value, axis, steps):
    count = lax.axis_size(axis)
    pairs = [(source, (source + steps) % count) for source in range(count)]
    return lax.ppermute(value, axis, pairs)


def dot(a, b, contract=((1,), (0,))):
    return lax.dot_general(a, b, (contract, ((), ())), preferred_element_type=jnp.float32)


def edge_kernel(
    grad_ref, window_ref, wt_ref, sel_ref, rad_ref, table_ref, rows_ref, feat_ref, radial_ref, weight_ref
):
    bf16 = jnp.bfloat16

    @pl.when(pl.program_id(0) == 0)
    def _():
        radial_ref[...] = jnp.zeros_like(radial_ref)

    sel = sel_ref[...]
    rad = rad_ref[...]
    table = table_ref[...]
    rows = rows_ref[...]
    radial_sum = jnp.zeros(radial_ref.shape, jnp.float32)
    basis_count = radial_ref.shape[0]
    for c in range(GROUP):
        wt = wt_ref[c]
        gathered = dot(window_ref[c], sel, ((0,), (0,))).astype(bf16)
        weighted = dot(rows, grad_ref[c])
        filt_grid = dot(wt, rad, ((0,), (0,)))
        feat_side = (weighted * filt_grid).astype(bf16)
        edge_grad = dot(table, feat_side).astype(bf16)
        feat_grid = dot(rows, gathered)
        filt_side = (weighted * feat_grid).astype(bf16)
        both = dot(jnp.concatenate([table, wt], axis=0), filt_side)
        filt_grad = both[:G_PAD].astype(bf16)
        radial_sum = (
            radial_sum + both[G_PAD : G_PAD + basis_count] + both[G_PAD + basis_count :]
        )
        feat_ref[c] = (dot(sel, edge_grad, ((1,), (1,))) * (1.0 / SAMPLES))[:, :G]
        weight_ref[c] = dot(rad[:basis_count], filt_grad, ((1,), (1,)))[:, :G]
    radial_ref[...] += radial_sum


def edge_call(grad, window, wt, sel, rad, table, rows):
    chan_count, _, edges = grad.shape
    sources = sel.shape[0]
    basis_count = wt.shape[1] // 2
    whole = lambda x: pl.BlockSpec(x.shape, lambda i: (0,) * x.ndim)
    grouped = lambda shape: pl.BlockSpec((GROUP,) + shape, lambda i: (i, 0, 0))
    return pl.pallas_call(
        edge_kernel,
        grid=(chan_count // GROUP,),
        in_specs=[
            grouped((G, edges)),
            grouped((sources, G)),
            grouped(wt.shape[1:]),
            whole(sel),
            whole(rad),
            whole(table),
            whole(rows),
        ],
        out_specs=[
            grouped((sources, G)),
            pl.BlockSpec((basis_count, edges), lambda i: (0, 0)),
            grouped((basis_count, G)),
        ],
        out_shape=[
            jax.ShapeDtypeStruct((chan_count, sources, G), jnp.float32),
            jax.ShapeDtypeStruct((basis_count, edges), jnp.float32),
            jax.ShapeDtypeStruct((chan_count, basis_count, G), jnp.float32),
        ],
        compiler_params=pltpu.CompilerParams(vmem_limit_bytes=40 * 1024 * 1024),
        name="edges",
    )(grad, window, wt, sel, rad, table, rows)


def local(feats, neighbors, counts, radial, filter_weight, message_grad):
    exact = basis_table()
    table = jnp.asarray(exact, jnp.bfloat16)
    rows = jnp.asarray(exact[:G].T, jnp.bfloat16)
    atom_count = lax.axis_size("atom")
    position = lax.axis_index("atom")
    block_len = feats.shape[3]
    chan_count = feats.shape[1]
    own_block = jnp.transpose(feats[0], (0, 2, 1))
    window = jnp.concatenate(
        [
            own_block if offset == 0 else passed_along(own_block, "atom", -offset)
            for offset in range(-REACH, REACH + 1)
        ],
        axis=1,
    )
    window_len = window.shape[1]
    sources = neighbors[0].reshape(-1)
    slot_index = (
        sources // block_len - position + REACH
    ) % atom_count * block_len + sources % block_len
    valid = (jnp.arange(SLOTS, dtype=jnp.int32)[None, :] < counts[0][:, None]).reshape(-1)
    selector = (
        (slot_index[None, :] == jnp.arange(window_len, dtype=jnp.int32)[:, None]) & valid[None, :]
    ).astype(jnp.bfloat16)
    radial_e = radial[0] * valid.astype(jnp.bfloat16)[None, :]
    radial_twice = jnp.concatenate([radial_e, radial_e], axis=0)
    weight_grid = jnp.einsum(
        "kcg,gp->ckp",
        filter_weight,
        table[:G],
        preferred_element_type=jnp.float32,
    )
    coarse = lax.reduce_precision(weight_grid, 8, 7)
    weight_parts = jnp.concatenate([coarse, weight_grid - coarse], axis=1).astype(jnp.bfloat16)
    window_grad, radial_local, weight_local = edge_call(
        message_grad[0], window, weight_parts, selector, radial_twice, table, rows
    )

    def block_of(offset):
        return window_grad[:, (offset + REACH) * block_len : (offset + REACH + 1) * block_len]

    returned_sum = block_of(0)
    for direction in (1, -1):
        carried = block_of(direction * REACH)
        for offset in range(REACH - 1, -1, -1):
            arrived = passed_along(carried, "atom", direction)
            if offset > 0:
                carried = arrived + block_of(direction * offset)
            else:
                returned_sum = returned_sum + arrived
    feat_grad = jnp.transpose(returned_sum, (0, 2, 1))[None]
    radial_grad = lax.psum(radial_local, "chan")[None] * (1.0 / SAMPLES)
    weight_summed = lax.psum(jnp.transpose(weight_local, (1, 0, 2)), ("atom", "rep"))
    weight_grad = weight_summed / (SAMPLES * atom_count * block_len * lax.axis_size("rep"))
    return (feat_grad, radial_grad, weight_grad)


def solution(mesh):
    placed = (
        P("rep", "chan", None, "atom"),
        P("rep", "atom", None),
        P("rep", "atom"),
        P("rep", None, "atom"),
        P(None, "chan", None),
        P("rep", "chan", None, "atom"),
    )
    return jax.shard_map(
        local,
        mesh=mesh,
        in_specs=placed,
        out_specs=(P("rep", "chan", None, "atom"), P("rep", None, "atom"), P(None, "chan", None)),
        check_vma=False,
    )
```

```python
import functools

import jax
import jax.numpy as jnp
import numpy as np
from jax import lax
from jax.experimental import pallas as pl
from jax.experimental.pallas import tpu as pltpu
from jax.sharding import PartitionSpec as P

BASIS = 9
POINTS = 13
SAMPLES = POINTS * POINTS
SAMPLES_PAD = -(-SAMPLES // 16) * 16
SLOTS = 32
REACH = 2
G = 81
G_PAD = 96
GROUP = 4


def basis_table():
    points = np.arange(POINTS) * (2.0 * np.pi / POINTS)
    degree_index = np.arange(BASIS)
    angles = ((degree_index + 1) // 2)[:, None] * points[None, :]
    single = np.where(
        degree_index[:, None] == 0,
        1.0,
        np.sqrt(2.0) * np.where(degree_index[:, None] % 2 == 1, np.cos(angles), np.sin(angles)),
    )
    product = (single[:, None, :, None] * single[None, :, None, :]).reshape(G, SAMPLES)
    padded = np.zeros((G_PAD, SAMPLES_PAD), np.float32)
    padded[:G, :SAMPLES] = product
    return padded


def passed_along(value, axis, steps):
    count = lax.axis_size(axis)
    pairs = [(source, (source + steps) % count) for source in range(count)]
    return lax.ppermute(value, axis, pairs)


def dot(a, b, contract=((1,), (0,))):
    return lax.dot_general(a, b, (contract, ((), ())), preferred_element_type=jnp.float32)


def feature_kernel(
    grad_ref, wt_ref, sel_ref, rad_ref, table_ref, rows_ref, grid_ref, own_ref, *sent_refs
):
    bf16 = jnp.bfloat16
    sel = sel_ref[...]
    rad = rad_ref[...]
    table = table_ref[...]
    rows = rows_ref[...]
    block_len = own_ref.shape[1]
    for c in range(GROUP):
        weighted = dot(rows, grad_ref[c])
        filt_grid = dot(wt_ref[c], rad)
        grid_ref[c] = weighted.astype(bf16)
        feat_side = (weighted * filt_grid).astype(bf16)
        edge_grad = dot(table, feat_side).astype(bf16)
        placed = (dot(sel, edge_grad, ((1,), (1,))) * (1.0 / SAMPLES))[:, :G]
        blocks = [
            placed[index * block_len : (index + 1) * block_len] for index in range(2 * REACH + 1)
        ]
        own_ref[c] = blocks.pop(REACH)
        for sent_ref, block in zip(sent_refs, blocks):
            sent_ref[c] = block.astype(bf16)


def filter_kernel(
    grid_ref, wt_ref, sel_ref, rad_ref, table_ref, rows_ref, *refs
):
    bf16 = jnp.bfloat16
    window_refs, (radial_ref, weight_ref) = refs[:-2], refs[-2:]

    @pl.when(pl.program_id(0) == 0)
    def _():
        radial_ref[...] = jnp.zeros_like(radial_ref)

    sel = sel_ref[...]
    table = table_ref[...]
    rows = rows_ref[...]
    basis_count = radial_ref.shape[0]
    rad = rad_ref[:basis_count]
    radial_sum = jnp.zeros(radial_ref.shape, jnp.float32)
    for c in range(GROUP):
        window = jnp.concatenate([ref[c] for ref in window_refs], axis=0)
        atom_grid = dot(rows, window, ((1,), (1,))).astype(bf16)
        feat_grid = dot(atom_grid, sel)
        filt_side = (grid_ref[c].astype(jnp.float32) * feat_grid).astype(bf16)
        both = dot(jnp.concatenate([table, wt_ref[c]], axis=0), filt_side)
        filt_grad = both[:G_PAD].astype(bf16)
        radial_sum = (
            radial_sum + both[G_PAD : G_PAD + basis_count] + both[G_PAD + basis_count :]
        )
        weight_ref[c] = dot(rad, filt_grad, ((1,), (1,)))[:, :G]
    radial_ref[...] += radial_sum


def whole(x):
    return pl.BlockSpec(x.shape, lambda i: (0,) * x.ndim)


def grouped(shape):
    return pl.BlockSpec((GROUP,) + tuple(shape), lambda i: (i, 0, 0))


def grid_call(kernel, name, out_shape, out_specs, split, shared, split_last=()):
    chan_count = split[0].shape[0]
    return pl.pallas_call(
        kernel,
        grid=(chan_count // GROUP,),
        in_specs=[grouped(x.shape[1:]) for x in split]
        + [whole(x) for x in shared]
        + [grouped(x.shape[1:]) for x in split_last],
        out_specs=out_specs,
        out_shape=out_shape,
        compiler_params=pltpu.CompilerParams(vmem_limit_bytes=54 * 1024 * 1024),
        cost_estimate=pl.CostEstimate(
            flops=chan_count * 160_000_000, bytes_accessed=16_000_000, transcendentals=0
        ),
        name=name,
    )(*split, *shared, *split_last)


def sum_kernel(
    weight_ref, radial_ref, weight_out, radial_out, parts, slots, send1, recv1, send2, recv2, send3, recv3
):
    atoms, reps, chans = (lax.axis_size(name) for name in ("atom", "rep", "chan"))
    atom, rep, chan = (lax.axis_index(name) for name in ("atom", "rep", "chan"))
    count = atoms * reps
    me = atom * reps + rep

    def member(step):
        index = lax.rem(me + step, count)
        return index, {"atom": index // reps, "chan": chan, "rep": lax.rem(index, reps)}

    def other(step):
        return {"atom": atom, "chan": lax.rem(chan + step, chans), "rep": rep}

    barrier = pltpu.get_barrier_semaphore()

    @pl.loop(1, count)
    def _(step):
        pl.semaphore_signal(
            barrier, inc=1, device_id=member(step)[1], device_id_type=pl.DeviceIdType.MESH
        )

    for step in range(1, chans):
        pl.semaphore_signal(
            barrier, inc=1, device_id=other(step), device_id_type=pl.DeviceIdType.MESH
        )
    pl.semaphore_wait(barrier, count - 1 + chans - 1)

    def chunk_copy(step):
        index, device = member(step)
        return pltpu.make_async_remote_copy(
            src_ref=weight_ref.at[index],
            dst_ref=parts.at[step],
            send_sem=send1.at[step],
            recv_sem=recv1.at[step],
            device_id=device,
            device_id_type=pl.DeviceIdType.MESH,
        )

    def radial_copy(step):
        return pltpu.make_async_remote_copy(
            src_ref=radial_ref,
            dst_ref=slots.at[chan],
            send_sem=send2.at[step],
            recv_sem=recv2.at[step],
            device_id=other(step),
            device_id_type=pl.DeviceIdType.MESH,
        )

    def total_copy(step):
        return pltpu.make_async_remote_copy(
            src_ref=weight_out.at[me],
            dst_ref=weight_out.at[me],
            send_sem=send3.at[step],
            recv_sem=recv3.at[step],
            device_id=member(step)[1],
            device_id_type=pl.DeviceIdType.MESH,
        )

    @pl.loop(1, count)
    def _(step):
        chunk_copy(step).start()

    for step in range(1, chans):
        radial_copy(step).start()
    slots[chan] = radial_ref[...]

    @pl.loop(1, count)
    def _(step):
        chunk_copy(step).wait_recv()

    total = weight_ref[me]
    for step in range(1, count):
        total = total + parts[step]
    weight_out[me] = total

    @pl.loop(1, count)
    def _(step):
        total_copy(step).start()

    for step in range(1, chans):
        radial_copy(step).wait()
    radial_total = slots[0]
    for index in range(1, chans):
        radial_total = radial_total + slots[index]
    radial_out[...] = radial_total * (1.0 / SAMPLES)

    @pl.loop(1, count)
    def _(step):
        chunk_copy(step).wait_send()
        total_copy(step).wait()


def sum_call(weight, radial):
    chans = lax.axis_size("chan")
    count = weight.shape[0]
    vmem = pl.BlockSpec(memory_space=pltpu.VMEM)
    sems = [pltpu.SemaphoreType.DMA((size,)) for size in (count, count, chans, chans, count, count)]
    return pl.pallas_call(
        sum_kernel,
        in_specs=[vmem, vmem],
        out_specs=[vmem, vmem],
        out_shape=[
            jax.ShapeDtypeStruct(weight.shape, jnp.float32),
            jax.ShapeDtypeStruct(radial.shape, jnp.float32),
        ],
        scratch_shapes=[
            pltpu.VMEM(weight.shape, jnp.float32),
            pltpu.VMEM((chans,) + radial.shape, jnp.float32),
        ]
        + sems,
        compiler_params=pltpu.CompilerParams(
            collective_id=0, has_side_effects=True, vmem_limit_bytes=16 * 1024 * 1024
        ),
        name="sums",
    )(weight, radial)


def local(feats, neighbors, counts, radial, filter_weight, message_grad):
    exact = basis_table()
    table = jnp.asarray(exact, jnp.bfloat16)
    rows = jnp.asarray(exact[:G].T, jnp.bfloat16)
    atom_count = lax.axis_size("atom")
    position = lax.axis_index("atom")
    block_len = feats.shape[3]
    chan_count = feats.shape[1]
    own_block = jnp.transpose(feats[0], (0, 2, 1))
    offsets = [offset for offset in range(-REACH, REACH + 1)]
    window = [
        own_block if offset == 0 else passed_along(own_block, "atom", -offset)
        for offset in offsets
    ]
    window_len = len(offsets) * block_len
    sources = neighbors[0].reshape(-1)
    slot_index = (
        sources // block_len - position + REACH
    ) % atom_count * block_len + sources % block_len
    valid = (jnp.arange(SLOTS, dtype=jnp.int32)[None, :] < counts[0][:, None]).reshape(-1)
    selector = (
        (slot_index[None, :] == jnp.arange(window_len, dtype=jnp.int32)[:, None]) & valid[None, :]
    ).astype(jnp.bfloat16)
    radial_e = radial[0] * valid.astype(jnp.bfloat16)[None, :]
    radial_twice = jnp.concatenate([radial_e, radial_e], axis=0)
    weight_grid = jnp.einsum(
        "kcg,gp->ckp", filter_weight, table[:G], preferred_element_type=jnp.float32
    )
    coarse = lax.reduce_precision(weight_grid, 8, 7)
    weight_parts = jnp.concatenate([coarse, weight_grid - coarse], axis=1).astype(jnp.bfloat16)
    basis_count = radial_e.shape[0]
    edges = radial_e.shape[1]
    block_shape = (chan_count, block_len, G)
    grid, own_grad, *outgoing = grid_call(
        feature_kernel,
        "feature_path",
        [
            jax.ShapeDtypeStruct((chan_count, SAMPLES_PAD, edges), jnp.bfloat16),
            jax.ShapeDtypeStruct(block_shape, jnp.float32),
        ]
        + [jax.ShapeDtypeStruct(block_shape, jnp.bfloat16)] * (2 * REACH),
        [grouped((SAMPLES_PAD, edges))] + [grouped(block_shape[1:])] * (2 * REACH + 1),
        [message_grad[0], jnp.transpose(weight_parts, (0, 2, 1))],
        [selector, radial_twice, table, rows],
    )
    arrived = [
        passed_along(block, "atom", offset)
        for offset, block in zip([o for o in offsets if o != 0], outgoing)
    ]
    radial_local, weight_local = grid_call(
        filter_kernel,
        "filter_path",
        [
            jax.ShapeDtypeStruct((basis_count, edges), jnp.float32),
            jax.ShapeDtypeStruct((chan_count, basis_count, G), jnp.float32),
        ],
        [
            pl.BlockSpec((basis_count, edges), lambda i: (0, 0)),
            grouped((basis_count, G)),
        ],
        [grid, weight_parts],
        [selector, radial_twice, table, rows],
        window,
    )
    sharers = atom_count * lax.axis_size("rep")
    weight_summed, radial_grad = sum_call(weight_local.reshape(sharers, -1, G), radial_local)
    weight_summed = jnp.transpose(weight_summed.reshape(chan_count, basis_count, G), (1, 0, 2))
    weight_grad = weight_summed * (1.0 / (SAMPLES * sharers * block_len))
    returned_sum = own_grad
    for block in arrived:
        returned_sum = returned_sum + block.astype(jnp.float32)
    feat_grad = jnp.transpose(returned_sum, (0, 2, 1))[None]
    return (feat_grad, radial_grad[None], weight_grad)


def solution(mesh):
    placed = (
        P("rep", "chan", None, "atom"),
        P("rep", "atom", None),
        P("rep", "atom"),
        P("rep", None, "atom"),
        P(None, "chan", None),
        P("rep", "chan", None, "atom"),
    )
    return jax.shard_map(
        local,
        mesh=mesh,
        in_specs=placed,
        out_specs=(P("rep", "chan", None, "atom"), P("rep", None, "atom"), P(None, "chan", None)),
        check_vma=False,
    )
```

```python
import functools

import jax
import jax.numpy as jnp
import numpy as np
from jax import lax
from jax.experimental import pallas as pl
from jax.experimental.pallas import tpu as pltpu
from jax.sharding import PartitionSpec as P

BASIS = 9
POINTS = 13
SAMPLES = POINTS * POINTS
SAMPLES_PAD = -(-SAMPLES // 16) * 16
SLOTS = 32
REACH = 2
G = 81
G_PAD = 96
GROUP = 16
SUB = 4
LANES = 128


def basis_table():
    points = np.arange(POINTS) * (2.0 * np.pi / POINTS)
    degree_index = np.arange(BASIS)
    angles = ((degree_index + 1) // 2)[:, None] * points[None, :]
    single = np.where(
        degree_index[:, None] == 0,
        1.0,
        np.sqrt(2.0) * np.where(degree_index[:, None] % 2 == 1, np.cos(angles), np.sin(angles)),
    )
    product = (single[:, None, :, None] * single[None, :, None, :]).reshape(G, SAMPLES)
    padded = np.zeros((G_PAD, SAMPLES_PAD), np.float32)
    padded[:G, :SAMPLES] = product
    return padded


def passed_along(value, axis, steps):
    count = lax.axis_size(axis)
    pairs = [(source, (source + steps) % count) for source in range(count)]
    return lax.ppermute(value, axis, pairs)


def dot(a, b, contract=((1,), (0,))):
    return lax.dot_general(a, b, (contract, ((), ())), preferred_element_type=jnp.float32)


def split_parts(value, axis):
    half = value.shape[axis] // 2
    coarse = value.astype(jnp.bfloat16).astype(jnp.float32)
    index = lax.broadcasted_iota(jnp.int32, value.shape, axis)
    return jnp.where(index < half, coarse, value - coarse).astype(jnp.bfloat16)


def feature_kernel(
    weight_ref, grad_ref, sel_ref, rad_ref, table_ref, rows_ref, grid_ref, own_ref, *refs
):
    bf16 = jnp.bfloat16
    sent_refs, spread = refs[:-1], refs[-1]
    rows = rows_ref[...]
    block_len = own_ref.shape[1]
    for tile in range(spread.shape[0]):
        spread[tile] = (
            grad_ref[:, :, tile * LANES : (tile + 1) * LANES]
            .astype(jnp.float32)
            .reshape(spread.shape[1:])
        )

    @pl.loop(0, GROUP // SUB)
    def _(batch):
        first = batch * SUB
        filters = [
            split_parts(dot(rows, weight_ref[first + c], ((1,), (1,))), 1) for c in range(SUB)
        ]
        filt_grid = dot(jnp.concatenate(filters, axis=0), rad_ref[...])
        sides = []
        for c in range(SUB):
            grad = jnp.concatenate(
                [
                    spread[tile, pl.ds(first + c, G, stride=GROUP), :].astype(bf16)
                    for tile in range(spread.shape[0])
                ],
                axis=1,
            )
            weighted = dot(rows, grad)
            grid_ref[first + c] = weighted.astype(bf16)
            sides.append(
                (weighted * filt_grid[c * SAMPLES_PAD : (c + 1) * SAMPLES_PAD]).astype(bf16)
            )
        summed = dot(jnp.concatenate(sides, axis=0), sel_ref[...]).astype(bf16)
        for c in range(SUB):
            placed = dot(table_ref[...], summed[c * SAMPLES_PAD : (c + 1) * SAMPLES_PAD])
            placed = (placed.T * (1.0 / SAMPLES))[:, :G]
            blocks = [
                placed[index * block_len : (index + 1) * block_len]
                for index in range(2 * REACH + 1)
            ]
            own_ref[first + c] = blocks.pop(REACH)
            for sent_ref, block in zip(sent_refs, blocks):
                sent_ref[first + c] = block.astype(bf16)


def filter_kernel(
    weight_ref, grid_ref, sel_ref, rad_ref, table_ref, rows_ref, rows_rest_ref, cols_ref, *refs
):
    bf16 = jnp.bfloat16
    window_refs, (radial_ref, out_ref) = refs[:-2], refs[-2:]
    basis_count = radial_ref.shape[0]

    @pl.when(pl.program_id(0) == 0)
    def _():
        radial_ref[...] = jnp.zeros_like(radial_ref)

    @pl.loop(0, GROUP // SUB)
    def _(batch):
        first = batch * SUB
        atom_grids = []
        for c in range(SUB):
            window = jnp.concatenate([ref[first + c] for ref in window_refs], axis=0)
            atom_grids.append(
                (
                    dot(rows_ref[...], window, ((1,), (1,)))
                    + dot(rows_rest_ref[...], window, ((1,), (1,)))
                ).astype(bf16)
            )
        feat_grid = dot(jnp.concatenate(atom_grids, axis=0), sel_ref[...])
        sides = [
            (
                grid_ref[first + c].astype(jnp.float32)
                * feat_grid[c * SAMPLES_PAD : (c + 1) * SAMPLES_PAD]
            ).astype(bf16)
            for c in range(SUB)
        ]
        summed = dot(jnp.concatenate(sides, axis=0), rad_ref[...]).astype(bf16)
        radial_sum = radial_ref[...]
        for c in range(SUB):
            filters = split_parts(dot(weight_ref[first + c], cols_ref[...]), 0)
            parts = dot(filters, sides[c])
            radial_sum = radial_sum + parts[:basis_count] + parts[basis_count:]
            placed = dot(table_ref[...], summed[c * SAMPLES_PAD : (c + 1) * SAMPLES_PAD])
            out_ref[first + c] = placed.T[:, :G]
        radial_ref[...] = radial_sum


def whole(x):
    return pl.BlockSpec(x.shape, lambda i: (0,) * x.ndim)


def grouped(shape):
    return pl.BlockSpec((GROUP,) + tuple(shape), lambda i: (i, 0, 0))


def grid_call(kernel, name, out_shape, out_specs, split, special, shared, split_last=(), scratch=()):
    chan_count = split[0].shape[0]
    return pl.pallas_call(
        kernel,
        grid=(chan_count // GROUP,),
        in_specs=[grouped(x.shape[1:]) for x in split]
        + [spec for _, spec in special]
        + [whole(x) for x in shared]
        + [grouped(x.shape[1:]) for x in split_last],
        out_specs=out_specs,
        out_shape=out_shape,
        scratch_shapes=list(scratch),
        compiler_params=pltpu.CompilerParams(vmem_limit_bytes=54 * 1024 * 1024),
        cost_estimate=pl.CostEstimate(
            flops=chan_count * 160_000_000, bytes_accessed=16_000_000, transcendentals=0
        ),
        name=name,
    )(*split, *[x for x, _ in special], *shared, *split_last)


def sum_kernel(
    weight_ref, radial_ref, weight_out, radial_out, parts, slots, send1, recv1, send2, recv2, send3, recv3
):
    atoms, reps, chans = (lax.axis_size(name) for name in ("atom", "rep", "chan"))
    atom, rep, chan = (lax.axis_index(name) for name in ("atom", "rep", "chan"))
    count = atoms * reps
    me = atom * reps + rep

    def member(step):
        index = lax.rem(me + step, count)
        return index, {"atom": index // reps, "chan": chan, "rep": lax.rem(index, reps)}

    def other(step):
        return {"atom": atom, "chan": lax.rem(chan + step, chans), "rep": rep}

    barrier = pltpu.get_barrier_semaphore()

    @pl.loop(1, count)
    def _(step):
        pl.semaphore_signal(
            barrier, inc=1, device_id=member(step)[1], device_id_type=pl.DeviceIdType.MESH
        )

    for step in range(1, chans):
        pl.semaphore_signal(
            barrier, inc=1, device_id=other(step), device_id_type=pl.DeviceIdType.MESH
        )
    pl.semaphore_wait(barrier, count - 1 + chans - 1)

    def chunk_copy(step):
        index, device = member(step)
        return pltpu.make_async_remote_copy(
            src_ref=weight_ref.at[index],
            dst_ref=parts.at[step],
            send_sem=send1.at[step],
            recv_sem=recv1.at[step],
            device_id=device,
            device_id_type=pl.DeviceIdType.MESH,
        )

    def radial_copy(step):
        return pltpu.make_async_remote_copy(
            src_ref=radial_ref,
            dst_ref=slots.at[chan],
            send_sem=send2.at[step],
            recv_sem=recv2.at[step],
            device_id=other(step),
            device_id_type=pl.DeviceIdType.MESH,
        )

    def total_copy(step):
        return pltpu.make_async_remote_copy(
            src_ref=weight_out.at[me],
            dst_ref=weight_out.at[me],
            send_sem=send3.at[step],
            recv_sem=recv3.at[step],
            device_id=member(step)[1],
            device_id_type=pl.DeviceIdType.MESH,
        )

    @pl.loop(1, count)
    def _(step):
        chunk_copy(step).start()

    for step in range(1, chans):
        radial_copy(step).start()
    slots[chan] = radial_ref[...]

    @pl.loop(1, count)
    def _(step):
        chunk_copy(step).wait_recv()

    total = weight_ref[me]
    for step in range(1, count):
        total = total + parts[step]
    weight_out[me] = total

    @pl.loop(1, count)
    def _(step):
        total_copy(step).start()

    for step in range(1, chans):
        radial_copy(step).wait()
    radial_total = slots[0]
    for index in range(1, chans):
        radial_total = radial_total + slots[index]
    radial_out[...] = radial_total * (1.0 / SAMPLES)

    @pl.loop(1, count)
    def _(step):
        chunk_copy(step).wait_send()
        total_copy(step).wait()


def sum_call(weight, radial):
    chans = lax.axis_size("chan")
    count = weight.shape[0]
    vmem = pl.BlockSpec(memory_space=pltpu.VMEM)
    sems = [pltpu.SemaphoreType.DMA((size,)) for size in (count, count, chans, chans, count, count)]
    return pl.pallas_call(
        sum_kernel,
        in_specs=[vmem, vmem],
        out_specs=[vmem, vmem],
        out_shape=[
            jax.ShapeDtypeStruct(weight.shape, jnp.float32),
            jax.ShapeDtypeStruct(radial.shape, jnp.float32),
        ],
        scratch_shapes=[
            pltpu.VMEM(weight.shape, jnp.float32),
            pltpu.VMEM((chans,) + radial.shape, jnp.float32),
        ]
        + sems,
        compiler_params=pltpu.CompilerParams(
            collective_id=0, has_side_effects=True, vmem_limit_bytes=16 * 1024 * 1024
        ),
        name="sums",
    )(weight, radial)


def local(feats, neighbors, counts, radial, filter_weight, message_grad):
    exact = basis_table()
    table = jnp.asarray(exact, jnp.bfloat16)
    rows_np = exact[:G].T.astype(jnp.bfloat16)
    rows = jnp.asarray(rows_np)
    atom_count = lax.axis_size("atom")
    position = lax.axis_index("atom")
    block_len = feats.shape[3]
    chan_count = feats.shape[1]
    own_block = jnp.transpose(feats[0], (0, 2, 1))
    offsets = [offset for offset in range(-REACH, REACH + 1)]
    window = [
        own_block if offset == 0 else passed_along(own_block, "atom", -offset)
        for offset in offsets
    ]
    window_len = len(offsets) * block_len
    sources = neighbors[0].reshape(-1)
    slot_index = (
        sources // block_len - position + REACH
    ) % atom_count * block_len + sources % block_len
    valid = (jnp.arange(SLOTS, dtype=jnp.int32)[None, :] < counts[0][:, None]).reshape(-1)
    slots = jnp.arange(window_len, dtype=jnp.int32)
    selector = ((slot_index[None, :] == slots[:, None]) & valid[None, :]).astype(jnp.bfloat16)
    selector_rows = ((slot_index[:, None] == slots[None, :]) & valid[:, None]).astype(jnp.bfloat16)
    radial_e = radial[0] * valid.astype(jnp.bfloat16)[None, :]
    radial_twice = jnp.concatenate([radial_e, radial_e], axis=0)
    rows_rest = jnp.asarray(exact[:G].T - np.asarray(rows_np, np.float32), jnp.bfloat16)
    weight_c = jnp.transpose(filter_weight, (1, 0, 2))
    weight_twice = jnp.concatenate([weight_c, weight_c], axis=1)
    basis_count = radial_e.shape[0]
    edges = radial_e.shape[1]
    block_shape = (chan_count, block_len, G)
    grid, own_grad, *outgoing = grid_call(
        feature_kernel,
        "feature_path",
        [
            jax.ShapeDtypeStruct((chan_count, SAMPLES_PAD, edges), jnp.bfloat16),
            jax.ShapeDtypeStruct(block_shape, jnp.float32),
        ]
        + [jax.ShapeDtypeStruct(block_shape, jnp.bfloat16)] * (2 * REACH),
        [grouped((SAMPLES_PAD, edges))] + [grouped(block_shape[1:])] * (2 * REACH + 1),
        [weight_twice],
        [
            (
                jnp.transpose(message_grad[0], (1, 0, 2)),
                pl.BlockSpec((G, GROUP, edges), lambda i: (0, i, 0)),
            )
        ],
        [selector_rows, radial_twice, table, rows],
        scratch=[pltpu.VMEM((edges // LANES, G * GROUP, LANES), jnp.float32)],
    )
    arrived = [
        passed_along(block, "atom", offset)
        for offset, block in zip([o for o in offsets if o != 0], outgoing)
    ]
    radial_local, weight_local = grid_call(
        filter_kernel,
        "filter_path",
        [
            jax.ShapeDtypeStruct((basis_count, edges), jnp.float32),
            jax.ShapeDtypeStruct((chan_count, basis_count, G), jnp.float32),
        ],
        [
            pl.BlockSpec((basis_count, edges), lambda i: (0, 0)),
            grouped((basis_count, G)),
        ],
        [weight_twice, grid],
        [],
        [selector, radial_e.T, table, rows, rows_rest, table[:G]],
        window,
    )
    sharers = atom_count * lax.axis_size("rep")
    weight_summed, radial_grad = sum_call(weight_local.reshape(sharers, -1, G), radial_local)
    weight_summed = jnp.transpose(weight_summed.reshape(chan_count, basis_count, G), (1, 0, 2))
    weight_grad = weight_summed * (1.0 / (SAMPLES * sharers * block_len))
    returned_sum = own_grad
    for block in arrived:
        returned_sum = returned_sum + block.astype(jnp.float32)
    feat_grad = jnp.transpose(returned_sum, (0, 2, 1))[None]
    return (feat_grad, radial_grad[None], weight_grad)


def solution(mesh):
    placed = (
        P("rep", "chan", None, "atom"),
        P("rep", "atom", None),
        P("rep", "atom"),
        P("rep", None, "atom"),
        P(None, "chan", None),
        P("rep", "chan", None, "atom"),
    )
    return jax.shard_map(
        local,
        mesh=mesh,
        in_specs=placed,
        out_specs=(P("rep", "chan", None, "atom"), P("rep", None, "atom"), P(None, "chan", None)),
        check_vma=False,
    )
```

```python
import functools

import jax
import jax.numpy as jnp
import numpy as np
from jax import lax
from jax.experimental import pallas as pl
from jax.experimental.pallas import tpu as pltpu
from jax.sharding import PartitionSpec as P

BASIS = 9
POINTS = 13
SAMPLES = POINTS * POINTS
SAMPLES_PAD = -(-SAMPLES // 16) * 16
SLOTS = 32
REACH = 2
G = 81
G_PAD = 96
GROUP = 16
SUB = 4
LANES = 128


def basis_table():
    points = np.arange(POINTS) * (2.0 * np.pi / POINTS)
    degree_index = np.arange(BASIS)
    angles = ((degree_index + 1) // 2)[:, None] * points[None, :]
    single = np.where(
        degree_index[:, None] == 0,
        1.0,
        np.sqrt(2.0) * np.where(degree_index[:, None] % 2 == 1, np.cos(angles), np.sin(angles)),
    )
    product = (single[:, None, :, None] * single[None, :, None, :]).reshape(G, SAMPLES)
    padded = np.zeros((G_PAD, SAMPLES_PAD), np.float32)
    padded[:G, :SAMPLES] = product
    return padded


def passed_along(value, axis, steps):
    count = lax.axis_size(axis)
    pairs = [(source, (source + steps) % count) for source in range(count)]
    return lax.ppermute(value, axis, pairs)


def dot(a, b, contract=((1,), (0,))):
    return lax.dot_general(a, b, (contract, ((), ())), preferred_element_type=jnp.float32)


def fill_filters(weight_ref, cols_ref, filt_rows):
    basis_count, group, coefficients = weight_ref.shape
    rows = dot(weight_ref[...].reshape(basis_count * group, coefficients), cols_ref[...])
    for half in range(filt_rows.shape[0]):
        filt_rows[half] = rows[:, half * LANES : (half + 1) * LANES]


def filters_of(filt_rows, channel):
    halves = [
        filt_rows[half, pl.ds(channel, filt_rows.shape[1] // GROUP, stride=GROUP), :]
        for half in range(filt_rows.shape[0])
    ]
    value = jnp.concatenate(halves, axis=1)
    coarse = value.astype(jnp.bfloat16).astype(jnp.float32)
    return jnp.concatenate([coarse, value - coarse], axis=0)


def selector(code_ref):
    code = code_ref[...]
    place = lax.broadcasted_iota(jnp.int32, (LANES, code.shape[1]), 0)
    return jnp.where(place == code, 1.0, 0.0)


def masked_radial(code_ref, rad_ref):
    return jnp.where(code_ref[...] >= 0, rad_ref[...].astype(jnp.float32), 0.0)


def feature_kernel(
    weight_ref, grad_ref, code_ref, rad_ref, table_ref, pair_ref, cols_ref, grid_ref, own_ref, *refs
):
    bf16 = jnp.bfloat16
    sent_refs, (spread, filt_rows, sel_t, rad_twice) = refs[:-4], refs[-4:]
    block_len = own_ref.shape[1]

    @pl.when(pl.program_id(0) == 0)
    def _():
        sel_t[...] = selector(code_ref).T.astype(bf16)
        rad = masked_radial(code_ref, rad_ref)
        rad_twice[...] = jnp.concatenate([rad, rad], axis=0).astype(bf16)
        spread[:, G * GROUP :, :] = jnp.zeros(
            (spread.shape[0], (G_PAD - G) * GROUP, LANES), jnp.float32
        )

    fill_filters(weight_ref, cols_ref, filt_rows)
    for tile in range(spread.shape[0]):
        spread[tile, : G * GROUP, :] = (
            grad_ref[:, :, tile * LANES : (tile + 1) * LANES]
            .astype(jnp.float32)
            .reshape(G * GROUP, LANES)
        )

    @pl.loop(0, GROUP // SUB)
    def _(batch):
        first = batch * SUB
        filters = [
            filters_of(filt_rows, first + c).T[:SAMPLES_PAD].astype(bf16) for c in range(SUB)
        ]
        filt_grid = dot(jnp.concatenate(filters, axis=0), rad_twice[...])
        sides = []
        for pair in range(0, SUB, 2):
            grads = [
                jnp.concatenate(
                    [
                        spread[tile, pl.ds(first + c, G_PAD, stride=GROUP), :].astype(bf16)
                        for tile in range(spread.shape[0])
                    ],
                    axis=1,
                )
                for c in (pair, pair + 1)
            ]
            both = dot(pair_ref[...], jnp.concatenate(grads, axis=0))
            for c in (pair, pair + 1):
                weighted = both[(c - pair) * SAMPLES_PAD : (c - pair + 1) * SAMPLES_PAD]
                grid_ref[first + c] = weighted.astype(bf16)
                sides.append(
                    (weighted * filt_grid[c * SAMPLES_PAD : (c + 1) * SAMPLES_PAD]).astype(bf16)
                )
        summed = dot(jnp.concatenate(sides, axis=0), sel_t[...]).astype(bf16)
        placed = dot(
            table_ref[...],
            jnp.concatenate(
                [summed[c * SAMPLES_PAD : (c + 1) * SAMPLES_PAD] for c in range(SUB)], axis=1
            ),
        ) * (1.0 / SAMPLES)
        for c in range(SUB):
            turned = placed[:, c * LANES : (c + 1) * LANES].T[:, :G]
            blocks = [
                turned[index * block_len : (index + 1) * block_len]
                for index in range(2 * REACH + 1)
            ]
            own_ref[first + c] = blocks.pop(REACH)
            for sent_ref, block in zip(sent_refs, blocks):
                sent_ref[first + c] = block.astype(bf16)


def filter_kernel(
    grid_ref, weight_ref, code_ref, rad_ref, table_t_ref, rows_ref, cols_ref, *refs
):
    bf16 = jnp.bfloat16
    window_refs, (radial_ref, out_ref, filt_rows, sel, rad_t) = refs[:-5], refs[-5:]
    basis_count = radial_ref.shape[0]

    @pl.when(pl.program_id(0) == 0)
    def _():
        radial_ref[...] = jnp.zeros_like(radial_ref)
        sel[...] = selector(code_ref).astype(bf16)
        rad_t[...] = masked_radial(code_ref, rad_ref).T.astype(bf16)

    fill_filters(weight_ref, cols_ref, filt_rows)
    block_len = window_refs[0].shape[1]
    rest = jnp.zeros((LANES - len(window_refs) * block_len, G), bf16)

    @pl.loop(0, GROUP // SUB)
    def _(batch):
        first = batch * SUB
        windows = []
        for c in range(SUB):
            windows += [ref[first + c] for ref in window_refs] + [rest]
        atom_grid = dot(rows_ref[...], jnp.concatenate(windows, axis=0), ((1,), (1,)))
        atom_grid = (atom_grid[:SAMPLES_PAD] + atom_grid[SAMPLES_PAD:]).astype(bf16)
        feat_grid = dot(
            jnp.concatenate(
                [atom_grid[:, c * LANES : (c + 1) * LANES] for c in range(SUB)], axis=0
            ),
            sel[...],
        )
        sides = jnp.concatenate(
            [
                (
                    grid_ref[first + c].astype(jnp.float32)
                    * feat_grid[c * SAMPLES_PAD : (c + 1) * SAMPLES_PAD]
                ).astype(bf16)
                for c in range(SUB)
            ],
            axis=0,
        )
        summed = dot(sides, rad_t[...])
        turned = jnp.concatenate(
            [summed[c * SAMPLES_PAD : (c + 1) * SAMPLES_PAD].T for c in range(SUB)], axis=0
        )
        placed = dot(turned.astype(bf16), table_t_ref[...])
        for c in range(SUB):
            out_ref[first + c] = placed[c * basis_count : (c + 1) * basis_count, :G]
        filters = jnp.concatenate(
            [filters_of(filt_rows, first + c)[:, :SAMPLES_PAD] for c in range(SUB)], axis=1
        )
        parts = dot(filters.astype(bf16), sides)
        radial_ref[...] += parts[:basis_count] + parts[basis_count:]


def whole(x):
    return pl.BlockSpec(x.shape, lambda i: (0,) * x.ndim)


def grouped(shape):
    return pl.BlockSpec((GROUP,) + tuple(shape), lambda i: (i, 0, 0))


def grid_call(
    kernel, name, chan_count, out_shape, out_specs, split, special, shared, split_last=(), scratch=()
):
    return pl.pallas_call(
        kernel,
        grid=(chan_count // GROUP,),
        in_specs=[grouped(x.shape[1:]) for x in split]
        + [spec for _, spec in special]
        + [whole(x) for x in shared]
        + [grouped(x.shape[1:]) for x in split_last],
        out_specs=out_specs,
        out_shape=out_shape,
        scratch_shapes=list(scratch),
        compiler_params=pltpu.CompilerParams(vmem_limit_bytes=54 * 1024 * 1024),
        cost_estimate=pl.CostEstimate(
            flops=chan_count * 160_000_000, bytes_accessed=16_000_000, transcendentals=0
        ),
        name=name,
    )(*split, *[x for x, _ in special], *shared, *split_last)


def sum_kernel(
    weight_ref, radial_ref, weight_out, radial_out, parts, slots, send1, recv1, send2, recv2, send3, recv3
):
    atoms, reps, chans = (lax.axis_size(name) for name in ("atom", "rep", "chan"))
    atom, rep, chan = (lax.axis_index(name) for name in ("atom", "rep", "chan"))
    count = atoms * reps
    me = atom * reps + rep

    def member(step):
        index = lax.rem(me + step, count)
        return index, {"atom": index // reps, "chan": chan, "rep": lax.rem(index, reps)}

    def other(step):
        return {"atom": atom, "chan": lax.rem(chan + step, chans), "rep": rep}

    barrier = pltpu.get_barrier_semaphore()

    @pl.loop(1, count)
    def _(step):
        pl.semaphore_signal(
            barrier, inc=1, device_id=member(step)[1], device_id_type=pl.DeviceIdType.MESH
        )

    for step in range(1, chans):
        pl.semaphore_signal(
            barrier, inc=1, device_id=other(step), device_id_type=pl.DeviceIdType.MESH
        )
    pl.semaphore_wait(barrier, count - 1 + chans - 1)

    def chunk_copy(step):
        index, device = member(step)
        return pltpu.make_async_remote_copy(
            src_ref=weight_ref.at[index],
            dst_ref=parts.at[step],
            send_sem=send1.at[step],
            recv_sem=recv1.at[step],
            device_id=device,
            device_id_type=pl.DeviceIdType.MESH,
        )

    def radial_copy(step):
        return pltpu.make_async_remote_copy(
            src_ref=radial_ref,
            dst_ref=slots.at[chan],
            send_sem=send2.at[step],
            recv_sem=recv2.at[step],
            device_id=other(step),
            device_id_type=pl.DeviceIdType.MESH,
        )

    def total_copy(step):
        return pltpu.make_async_remote_copy(
            src_ref=weight_out.at[me],
            dst_ref=weight_out.at[me],
            send_sem=send3.at[step],
            recv_sem=recv3.at[step],
            device_id=member(step)[1],
            device_id_type=pl.DeviceIdType.MESH,
        )

    @pl.loop(1, count)
    def _(step):
        chunk_copy(step).start()

    for step in range(1, chans):
        radial_copy(step).start()
    slots[chan] = radial_ref[...]

    @pl.loop(1, count)
    def _(step):
        chunk_copy(step).wait_recv()

    total = weight_ref[me]
    for step in range(1, count):
        total = total + parts[step]
    weight_out[me] = total

    @pl.loop(1, count)
    def _(step):
        total_copy(step).start()

    for step in range(1, chans):
        radial_copy(step).wait()
    radial_total = slots[0]
    for index in range(1, chans):
        radial_total = radial_total + slots[index]
    radial_out[...] = radial_total * (1.0 / SAMPLES)

    @pl.loop(1, count)
    def _(step):
        chunk_copy(step).wait_send()
        total_copy(step).wait()


def sum_call(weight, radial):
    chans = lax.axis_size("chan")
    count = weight.shape[0]
    vmem = pl.BlockSpec(memory_space=pltpu.VMEM)
    sems = [pltpu.SemaphoreType.DMA((size,)) for size in (count, count, chans, chans, count, count)]
    return pl.pallas_call(
        sum_kernel,
        in_specs=[vmem, vmem],
        out_specs=[vmem, vmem],
        out_shape=[
            jax.ShapeDtypeStruct(weight.shape, jnp.float32),
            jax.ShapeDtypeStruct(radial.shape, jnp.float32),
        ],
        scratch_shapes=[
            pltpu.VMEM(weight.shape, jnp.float32),
            pltpu.VMEM((chans,) + radial.shape, jnp.float32),
        ]
        + sems,
        compiler_params=pltpu.CompilerParams(
            collective_id=0, has_side_effects=True, vmem_limit_bytes=16 * 1024 * 1024
        ),
        name="sums",
    )(weight, radial)


def local(feats, neighbors, counts, radial, filter_weight, message_grad):
    exact = basis_table()
    rounded = exact.astype(jnp.bfloat16)
    remainder = (exact - rounded.astype(np.float32)).astype(jnp.bfloat16)
    table = jnp.asarray(rounded)
    table_t = jnp.asarray(rounded.T)
    pair_rows = jnp.asarray(np.kron(np.eye(2, dtype=np.float32), rounded.T.astype(np.float32)), jnp.bfloat16)
    split_rows = jnp.asarray(np.concatenate([rounded[:G].T, remainder[:G].T], axis=0))
    columns = jnp.asarray(np.pad(rounded[:G], ((0, 0), (0, -SAMPLES_PAD % LANES))))
    atom_count = lax.axis_size("atom")
    position = lax.axis_index("atom")
    block_len = feats.shape[3]
    chan_count = feats.shape[1]
    own_block = jnp.transpose(feats[0], (0, 2, 1))
    offsets = [offset for offset in range(-REACH, REACH + 1)]
    window = [
        own_block if offset == 0 else passed_along(own_block, "atom", -offset)
        for offset in offsets
    ]
    sources = neighbors[0].reshape(-1)
    slot_index = (
        sources // block_len - position + REACH
    ) % atom_count * block_len + sources % block_len
    valid = (jnp.arange(SLOTS, dtype=jnp.int32)[None, :] < counts[0][:, None]).reshape(-1)
    code = jnp.where(valid, slot_index, -1)[None, :]
    radial_e = radial[0]
    basis_count = radial_e.shape[0]
    edges = radial_e.shape[1]
    block_shape = (chan_count, block_len, G)
    weight_spec = pl.BlockSpec((basis_count, GROUP, G), lambda i: (0, i, 0))
    filter_scratch = pltpu.VMEM(
        (-(-SAMPLES_PAD // LANES), basis_count * GROUP, LANES), jnp.float32
    )
    grid, own_grad, *outgoing = grid_call(
        feature_kernel,
        "feature_path",
        chan_count,
        [
            jax.ShapeDtypeStruct((chan_count, SAMPLES_PAD, edges), jnp.bfloat16),
            jax.ShapeDtypeStruct(block_shape, jnp.float32),
        ]
        + [jax.ShapeDtypeStruct(block_shape, jnp.bfloat16)] * (2 * REACH),
        [grouped((SAMPLES_PAD, edges))] + [grouped(block_shape[1:])] * (2 * REACH + 1),
        [],
        [
            (filter_weight, weight_spec),
            (
                jnp.transpose(message_grad[0], (1, 0, 2)),
                pl.BlockSpec((G, GROUP, edges), lambda i: (0, i, 0)),
            )
        ],
        [code, radial_e, table, pair_rows, columns],
        scratch=[
            pltpu.VMEM((edges // LANES, G_PAD * GROUP, LANES), jnp.float32),
            filter_scratch,
            pltpu.VMEM((edges, LANES), jnp.bfloat16),
            pltpu.VMEM((2 * basis_count, edges), jnp.bfloat16),
        ],
    )
    arrived = [
        passed_along(block, "atom", offset)
        for offset, block in zip([o for o in offsets if o != 0], outgoing)
    ]
    radial_local, weight_local = grid_call(
        filter_kernel,
        "filter_path",
        chan_count,
        [
            jax.ShapeDtypeStruct((basis_count, edges), jnp.float32),
            jax.ShapeDtypeStruct((chan_count, basis_count, G), jnp.float32),
        ],
        [
            pl.BlockSpec((basis_count, edges), lambda i: (0, 0)),
            grouped((basis_count, G)),
        ],
        [grid],
        [(filter_weight, weight_spec)],
        [code, radial_e, table_t, split_rows, columns],
        window,
        scratch=[
            filter_scratch,
            pltpu.VMEM((LANES, edges), jnp.bfloat16),
            pltpu.VMEM((edges, basis_count), jnp.bfloat16),
        ],
    )
    sharers = atom_count * lax.axis_size("rep")
    weight_summed, radial_grad = sum_call(weight_local.reshape(sharers, -1, G), radial_local)
    weight_summed = jnp.transpose(weight_summed.reshape(chan_count, basis_count, G), (1, 0, 2))
    weight_grad = weight_summed * (1.0 / (SAMPLES * sharers * block_len))
    returned_sum = own_grad
    for block in arrived:
        returned_sum = returned_sum + block.astype(jnp.float32)
    feat_grad = jnp.transpose(returned_sum, (0, 2, 1))[None]
    return (feat_grad, radial_grad[None], weight_grad)


def solution(mesh):
    placed = (
        P("rep", "chan", None, "atom"),
        P("rep", "atom", None),
        P("rep", "atom"),
        P("rep", None, "atom"),
        P(None, "chan", None),
        P("rep", "chan", None, "atom"),
    )
    return jax.shard_map(
        local,
        mesh=mesh,
        in_specs=placed,
        out_specs=(P("rep", "chan", None, "atom"), P("rep", None, "atom"), P(None, "chan", None)),
        check_vma=False,
    )
```

```python
import functools

import jax
import jax.numpy as jnp
import numpy as np
from jax import lax
from jax.experimental import pallas as pl
from jax.experimental.pallas import tpu as pltpu
from jax.sharding import PartitionSpec as P

BASIS = 9
POINTS = 13
SAMPLES = POINTS * POINTS
SAMPLES_PAD = -(-SAMPLES // 16) * 16
SLOTS = 32
REACH = 2
G = 81
G_PAD = 96
GROUP = 16
SUB = 8
LANES = 128


def basis_table():
    points = np.arange(POINTS) * (2.0 * np.pi / POINTS)
    degree_index = np.arange(BASIS)
    angles = ((degree_index + 1) // 2)[:, None] * points[None, :]
    single = np.where(
        degree_index[:, None] == 0,
        1.0,
        np.sqrt(2.0) * np.where(degree_index[:, None] % 2 == 1, np.cos(angles), np.sin(angles)),
    )
    product = (single[:, None, :, None] * single[None, :, None, :]).reshape(G, SAMPLES)
    padded = np.zeros((G_PAD, SAMPLES_PAD), np.float32)
    padded[:G, :SAMPLES] = product
    return padded


def passed_along(value, axis, steps):
    count = lax.axis_size(axis)
    pairs = [(source, (source + steps) % count) for source in range(count)]
    return lax.ppermute(value, axis, pairs)


def dot(a, b, contract=((1,), (0,))):
    return lax.dot_general(a, b, (contract, ((), ())), preferred_element_type=jnp.float32)


def fill_filters(weight_ref, cols_ref, filt_rows):
    basis_count, group, coefficients = weight_ref.shape
    rows = dot(weight_ref[...].reshape(basis_count * group, coefficients), cols_ref[...])
    for half in range(filt_rows.shape[0]):
        filt_rows[half] = rows[:, half * LANES : (half + 1) * LANES]


def filters_of(filt_rows, channel):
    halves = [
        filt_rows[half, pl.ds(channel, filt_rows.shape[1] // GROUP, stride=GROUP), :]
        for half in range(filt_rows.shape[0])
    ]
    value = jnp.concatenate(halves, axis=1)
    coarse = value.astype(jnp.bfloat16).astype(jnp.float32)
    return jnp.concatenate([coarse, value - coarse], axis=0)


def selector(code_ref):
    code = code_ref[...]
    place = lax.broadcasted_iota(jnp.int32, (LANES, code.shape[1]), 0)
    return jnp.where(place == code, 1.0, 0.0)


def masked_radial(code_ref, rad_ref):
    return jnp.where(code_ref[...] >= 0, rad_ref[...].astype(jnp.float32), 0.0)


def feature_kernel(
    weight_ref, grad_ref, code_ref, rad_ref, table_ref, pair_ref, cols_ref, grid_ref, own_ref, *refs
):
    bf16 = jnp.bfloat16
    sent_refs, (spread, filt_rows, sel_t, rad_twice) = refs[:-4], refs[-4:]
    block_len = own_ref.shape[1]

    @pl.when(pl.program_id(0) == 0)
    def _():
        sel_t[...] = selector(code_ref).T.astype(bf16)
        rad = masked_radial(code_ref, rad_ref)
        rad_twice[...] = jnp.concatenate([rad, rad], axis=0).astype(bf16)
        spread[:, G * GROUP :, :] = jnp.zeros(
            (spread.shape[0], (G_PAD - G) * GROUP, LANES), jnp.float32
        )

    fill_filters(weight_ref, cols_ref, filt_rows)
    for tile in range(spread.shape[0]):
        spread[tile, : G * GROUP, :] = (
            grad_ref[:, :, tile * LANES : (tile + 1) * LANES]
            .astype(jnp.float32)
            .reshape(G * GROUP, LANES)
        )

    @pl.loop(0, GROUP // SUB)
    def _(batch):
        first = batch * SUB
        filters = [
            filters_of(filt_rows, first + c).T[:SAMPLES_PAD].astype(bf16) for c in range(SUB)
        ]
        filt_grid = dot(jnp.concatenate(filters, axis=0), rad_twice[...])
        sides = []
        for pair in range(0, SUB, 2):
            grads = [
                jnp.concatenate(
                    [
                        spread[tile, pl.ds(first + c, G_PAD, stride=GROUP), :].astype(bf16)
                        for tile in range(spread.shape[0])
                    ],
                    axis=1,
                )
                for c in (pair, pair + 1)
            ]
            both = dot(pair_ref[...], jnp.concatenate(grads, axis=0))
            for c in (pair, pair + 1):
                weighted = both[(c - pair) * SAMPLES_PAD : (c - pair + 1) * SAMPLES_PAD]
                grid_ref[first + c] = weighted.astype(bf16)
                sides.append(
                    (weighted * filt_grid[c * SAMPLES_PAD : (c + 1) * SAMPLES_PAD]).astype(bf16)
                )
        summed = dot(jnp.concatenate(sides, axis=0), sel_t[...]).astype(bf16)
        placed = dot(
            table_ref[...],
            jnp.concatenate(
                [summed[c * SAMPLES_PAD : (c + 1) * SAMPLES_PAD] for c in range(SUB)], axis=1
            ),
        ) * (1.0 / SAMPLES)
        for c in range(SUB):
            turned = placed[:, c * LANES : (c + 1) * LANES].T[:, :G]
            blocks = [
                turned[index * block_len : (index + 1) * block_len]
                for index in range(2 * REACH + 1)
            ]
            own_ref[first + c] = blocks.pop(REACH)
            for sent_ref, block in zip(sent_refs, blocks):
                sent_ref[first + c] = block.astype(bf16)


def filter_kernel(
    grid_ref, weight_ref, code_ref, rad_ref, table_t_ref, rows_ref, cols_ref, *refs
):
    bf16 = jnp.bfloat16
    window_refs, (radial_ref, out_ref, filt_rows, sel, rad_t) = refs[:-5], refs[-5:]
    basis_count = radial_ref.shape[0]

    @pl.when(pl.program_id(0) == 0)
    def _():
        radial_ref[...] = jnp.zeros_like(radial_ref)
        sel[...] = selector(code_ref).astype(bf16)
        rad_t[...] = masked_radial(code_ref, rad_ref).T.astype(bf16)

    fill_filters(weight_ref, cols_ref, filt_rows)
    block_len = window_refs[0].shape[1]
    rest = jnp.zeros((LANES - len(window_refs) * block_len, G), bf16)

    @pl.loop(0, GROUP // SUB)
    def _(batch):
        first = batch * SUB
        windows = []
        for c in range(SUB):
            windows += [ref[first + c] for ref in window_refs] + [rest]
        atom_grid = dot(rows_ref[...], jnp.concatenate(windows, axis=0), ((1,), (1,)))
        atom_grid = (atom_grid[:SAMPLES_PAD] + atom_grid[SAMPLES_PAD:]).astype(bf16)
        feat_grid = dot(
            jnp.concatenate(
                [atom_grid[:, c * LANES : (c + 1) * LANES] for c in range(SUB)], axis=0
            ),
            sel[...],
        )
        sides = jnp.concatenate(
            [
                (
                    grid_ref[first + c].astype(jnp.float32)
                    * feat_grid[c * SAMPLES_PAD : (c + 1) * SAMPLES_PAD]
                ).astype(bf16)
                for c in range(SUB)
            ],
            axis=0,
        )
        summed = dot(sides, rad_t[...])
        turned = jnp.concatenate(
            [summed[c * SAMPLES_PAD : (c + 1) * SAMPLES_PAD].T for c in range(SUB)], axis=0
        )
        placed = dot(turned.astype(bf16), table_t_ref[...])
        span = SUB * basis_count
        out_ref[pl.ds(pl.multiple_of(batch * span, span), span), :] = placed[:, :G].astype(bf16)
        filters = jnp.concatenate(
            [filters_of(filt_rows, first + c)[:, :SAMPLES_PAD] for c in range(SUB)], axis=1
        )
        parts = dot(filters.astype(bf16), sides)
        radial_ref[...] += parts[:basis_count] + parts[basis_count:]


def whole(x):
    return pl.BlockSpec(x.shape, lambda i: (0,) * x.ndim)


def grouped(shape):
    return pl.BlockSpec((GROUP,) + tuple(shape), lambda i: (i, 0, 0))


def grid_call(
    kernel, name, chan_count, out_shape, out_specs, split, special, shared, split_last=(), scratch=()
):
    return pl.pallas_call(
        kernel,
        grid=(chan_count // GROUP,),
        in_specs=[grouped(x.shape[1:]) for x in split]
        + [spec for _, spec in special]
        + [whole(x) for x in shared]
        + [grouped(x.shape[1:]) for x in split_last],
        out_specs=out_specs,
        out_shape=out_shape,
        scratch_shapes=list(scratch),
        compiler_params=pltpu.CompilerParams(vmem_limit_bytes=54 * 1024 * 1024),
        cost_estimate=pl.CostEstimate(
            flops=chan_count * 160_000_000, bytes_accessed=16_000_000, transcendentals=0
        ),
        name=name,
    )(*split, *[x for x, _ in special], *shared, *split_last)


def sum_kernel(
    weight_ref, radial_ref, weight_out, radial_out, parts, slots, send1, recv1, send2, recv2, send3, recv3, own
):
    atoms, reps, chans = (lax.axis_size(name) for name in ("atom", "rep", "chan"))
    atom, rep, chan = (lax.axis_index(name) for name in ("atom", "rep", "chan"))
    count = atoms * reps
    me = atom * reps + rep

    def member(step):
        index = lax.rem(me + step, count)
        return index, {"atom": index // reps, "chan": chan, "rep": lax.rem(index, reps)}

    def other(step):
        return {"atom": atom, "chan": lax.rem(chan + step, chans), "rep": rep}

    own_chunk = pltpu.make_async_copy(weight_ref.at[me], parts.at[0], own.at[0])
    own_radial = pltpu.make_async_copy(radial_ref, slots.at[chan], own.at[1])
    own_chunk.start()
    own_radial.start()
    barrier = pltpu.get_barrier_semaphore()

    @pl.loop(1, count)
    def _(step):
        pl.semaphore_signal(
            barrier, inc=1, device_id=member(step)[1], device_id_type=pl.DeviceIdType.MESH
        )

    for step in range(1, chans):
        pl.semaphore_signal(
            barrier, inc=1, device_id=other(step), device_id_type=pl.DeviceIdType.MESH
        )
    pl.semaphore_wait(barrier, count - 1 + chans - 1)

    def chunk_copy(step):
        index, device = member(step)
        return pltpu.make_async_remote_copy(
            src_ref=weight_ref.at[index],
            dst_ref=parts.at[step],
            send_sem=send1.at[step],
            recv_sem=recv1.at[step],
            device_id=device,
            device_id_type=pl.DeviceIdType.MESH,
        )

    def radial_copy(step):
        return pltpu.make_async_remote_copy(
            src_ref=radial_ref,
            dst_ref=slots.at[chan],
            send_sem=send2.at[step],
            recv_sem=recv2.at[step],
            device_id=other(step),
            device_id_type=pl.DeviceIdType.MESH,
        )

    def total_copy(step):
        return pltpu.make_async_remote_copy(
            src_ref=weight_out.at[me],
            dst_ref=weight_out.at[me],
            send_sem=send3.at[step],
            recv_sem=recv3.at[step],
            device_id=member(step)[1],
            device_id_type=pl.DeviceIdType.MESH,
        )

    @pl.loop(1, count)
    def _(step):
        chunk_copy(step).start()

    for step in range(1, chans):
        radial_copy(step).start()

    @pl.loop(1, count)
    def _(step):
        chunk_copy(step).wait_recv()

    own_chunk.wait()
    total = parts[0].astype(jnp.float32)
    for step in range(1, count):
        total = total + parts[step].astype(jnp.float32)
    weight_out[me] = total.astype(weight_out.dtype)

    @pl.loop(1, count)
    def _(step):
        total_copy(step).start()

    for step in range(1, chans):
        radial_copy(step).wait()
    own_radial.wait()
    radial_total = slots[0]
    for index in range(1, chans):
        radial_total = radial_total + slots[index]
    radial_out[...] = radial_total * (1.0 / SAMPLES)

    @pl.loop(1, count)
    def _(step):
        chunk_copy(step).wait_send()
        total_copy(step).wait()


def sum_call(weight, radial):
    chans = lax.axis_size("chan")
    count = weight.shape[0]
    vmem = pl.BlockSpec(memory_space=pltpu.VMEM)
    anywhere = pl.BlockSpec(memory_space=pl.ANY)
    sizes = (count, count, chans, chans, count, count, 2)
    sems = [pltpu.SemaphoreType.DMA((size,)) for size in sizes]
    return pl.pallas_call(
        sum_kernel,
        in_specs=[anywhere, anywhere],
        out_specs=[vmem, vmem],
        out_shape=[
            jax.ShapeDtypeStruct(weight.shape, weight.dtype),
            jax.ShapeDtypeStruct(radial.shape, jnp.float32),
        ],
        scratch_shapes=[
            pltpu.VMEM(weight.shape, weight.dtype),
            pltpu.VMEM((chans,) + radial.shape, jnp.float32),
        ]
        + sems,
        compiler_params=pltpu.CompilerParams(collective_id=0, has_side_effects=True),
        name="sums",
    )(weight, radial)


def local(feats, neighbors, counts, radial, filter_weight, message_grad):
    exact = basis_table()
    rounded = exact.astype(jnp.bfloat16)
    remainder = (exact - rounded.astype(np.float32)).astype(jnp.bfloat16)
    table = jnp.asarray(rounded)
    table_t = jnp.asarray(rounded.T)
    pair_rows = jnp.asarray(np.kron(np.eye(2, dtype=np.float32), rounded.T.astype(np.float32)), jnp.bfloat16)
    split_rows = jnp.asarray(np.concatenate([rounded[:G].T, remainder[:G].T], axis=0))
    columns = jnp.asarray(np.pad(rounded[:G], ((0, 0), (0, -SAMPLES_PAD % LANES))))
    atom_count = lax.axis_size("atom")
    position = lax.axis_index("atom")
    block_len = feats.shape[3]
    chan_count = feats.shape[1]
    own_block = jnp.transpose(feats[0], (0, 2, 1))
    offsets = [offset for offset in range(-REACH, REACH + 1)]
    window = [
        own_block if offset == 0 else passed_along(own_block, "atom", -offset)
        for offset in offsets
    ]
    sources = neighbors[0].reshape(-1)
    slot_index = (
        sources // block_len - position + REACH
    ) % atom_count * block_len + sources % block_len
    valid = (jnp.arange(SLOTS, dtype=jnp.int32)[None, :] < counts[0][:, None]).reshape(-1)
    code = jnp.where(valid, slot_index, -1)[None, :]
    radial_e = radial[0]
    basis_count = radial_e.shape[0]
    edges = radial_e.shape[1]
    block_shape = (chan_count, block_len, G)
    weight_spec = pl.BlockSpec((basis_count, GROUP, G), lambda i: (0, i, 0))
    filter_scratch = pltpu.VMEM(
        (-(-SAMPLES_PAD // LANES), basis_count * GROUP, LANES), jnp.float32
    )
    grid, own_grad, *outgoing = grid_call(
        feature_kernel,
        "feature_path",
        chan_count,
        [
            jax.ShapeDtypeStruct((chan_count, SAMPLES_PAD, edges), jnp.bfloat16),
            jax.ShapeDtypeStruct(block_shape, jnp.float32),
        ]
        + [jax.ShapeDtypeStruct(block_shape, jnp.bfloat16)] * (2 * REACH),
        [grouped((SAMPLES_PAD, edges))] + [grouped(block_shape[1:])] * (2 * REACH + 1),
        [],
        [
            (filter_weight, weight_spec),
            (
                jnp.transpose(message_grad[0], (1, 0, 2)),
                pl.BlockSpec((G, GROUP, edges), lambda i: (0, i, 0)),
            )
        ],
        [code, radial_e, table, pair_rows, columns],
        scratch=[
            pltpu.VMEM((edges // LANES, G_PAD * GROUP, LANES), jnp.float32),
            filter_scratch,
            pltpu.VMEM((edges, LANES), jnp.bfloat16),
            pltpu.VMEM((2 * basis_count, edges), jnp.bfloat16),
        ],
    )
    arrived = [
        passed_along(block, "atom", offset)
        for offset, block in zip([o for o in offsets if o != 0], outgoing)
    ]
    radial_local, weight_local = grid_call(
        filter_kernel,
        "filter_path",
        chan_count,
        [
            jax.ShapeDtypeStruct((basis_count, edges), jnp.float32),
            jax.ShapeDtypeStruct((chan_count * basis_count, G), jnp.bfloat16),
        ],
        [
            pl.BlockSpec((basis_count, edges), lambda i: (0, 0)),
            pl.BlockSpec((GROUP * basis_count, G), lambda i: (i, 0)),
        ],
        [grid],
        [(filter_weight, weight_spec)],
        [code, radial_e, table_t, split_rows, columns],
        window,
        scratch=[
            filter_scratch,
            pltpu.VMEM((LANES, edges), jnp.bfloat16),
            pltpu.VMEM((edges, basis_count), jnp.bfloat16),
        ],
    )
    sharers = atom_count * lax.axis_size("rep")
    weight_summed, radial_grad = sum_call(weight_local.reshape(sharers, -1, G), radial_local)
    weight_summed = jnp.transpose(weight_summed.reshape(chan_count, basis_count, G), (1, 0, 2))
    weight_grad = weight_summed.astype(jnp.float32) * (1.0 / (SAMPLES * sharers * block_len))
    returned_sum = own_grad
    for block in arrived:
        returned_sum = returned_sum + block.astype(jnp.float32)
    feat_grad = jnp.transpose(returned_sum, (0, 2, 1))[None]
    return (feat_grad, radial_grad[None], weight_grad)


def solution(mesh):
    placed = (
        P("rep", "chan", None, "atom"),
        P("rep", "atom", None),
        P("rep", "atom"),
        P("rep", None, "atom"),
        P(None, "chan", None),
        P("rep", "chan", None, "atom"),
    )
    return jax.shard_map(
        local,
        mesh=mesh,
        in_specs=placed,
        out_specs=(P("rep", "chan", None, "atom"), P("rep", None, "atom"), P(None, "chan", None)),
        check_vma=False,
    )
```

```python
import functools

import jax
import jax.numpy as jnp
import numpy as np
from jax import lax
from jax.experimental import pallas as pl
from jax.experimental.pallas import tpu as pltpu
from jax.sharding import PartitionSpec as P

BASIS = 9
POINTS = 13
SAMPLES = POINTS * POINTS
SAMPLES_PAD = -(-SAMPLES // 16) * 16
SLOTS = 32
REACH = 2
G = 81
G_PAD = 96
GROUP = 16
SUB = 16
LANES = 128


def basis_table():
    points = np.arange(POINTS) * (2.0 * np.pi / POINTS)
    degree_index = np.arange(BASIS)
    angles = ((degree_index + 1) // 2)[:, None] * points[None, :]
    single = np.where(
        degree_index[:, None] == 0,
        1.0,
        np.sqrt(2.0) * np.where(degree_index[:, None] % 2 == 1, np.cos(angles), np.sin(angles)),
    )
    product = (single[:, None, :, None] * single[None, :, None, :]).reshape(G, SAMPLES)
    padded = np.zeros((G_PAD, SAMPLES_PAD), np.float32)
    padded[:G, :SAMPLES] = product
    return padded


def passed_along(value, axis, steps):
    count = lax.axis_size(axis)
    pairs = [(source, (source + steps) % count) for source in range(count)]
    return lax.ppermute(value, axis, pairs)


def dot(a, b, contract=((1,), (0,))):
    return lax.dot_general(a, b, (contract, ((), ())), preferred_element_type=jnp.float32)


def fill_filters(weight_ref, cols_ref, filt_rows):
    basis_count, group, coefficients = weight_ref.shape
    rows = dot(weight_ref[...].reshape(basis_count * group, coefficients), cols_ref[...])
    for half in range(filt_rows.shape[0]):
        filt_rows[half] = rows[:, half * LANES : (half + 1) * LANES]


def filters_of(filt_rows, channel):
    halves = [
        filt_rows[half, pl.ds(channel, filt_rows.shape[1] // GROUP, stride=GROUP), :]
        for half in range(filt_rows.shape[0])
    ]
    value = jnp.concatenate(halves, axis=1)
    coarse = value.astype(jnp.bfloat16).astype(jnp.float32)
    return jnp.concatenate([coarse, value - coarse], axis=0)


def selector(code_ref):
    code = code_ref[...]
    place = lax.broadcasted_iota(jnp.int32, (LANES, code.shape[1]), 0)
    return jnp.where(place == code, 1.0, 0.0)


def masked_radial(code_ref, rad_ref):
    return jnp.where(code_ref[...] >= 0, rad_ref[...].astype(jnp.float32), 0.0)


def feature_kernel(
    weight_ref, grad_ref, code_ref, rad_ref, table_ref, pair_ref, cols_ref, grid_ref, own_ref, *refs
):
    bf16 = jnp.bfloat16
    sent_refs, (spread, filt_rows, sel_t, rad_twice) = refs[:-4], refs[-4:]
    block_len = own_ref.shape[1]

    @pl.when(pl.program_id(0) == 0)
    def _():
        sel_t[...] = selector(code_ref).T.astype(bf16)
        rad = masked_radial(code_ref, rad_ref)
        rad_twice[...] = jnp.concatenate([rad, rad], axis=0).astype(bf16)
        spread[:, G * GROUP :, :] = jnp.zeros(
            (spread.shape[0], (G_PAD - G) * GROUP, LANES), jnp.float32
        )

    fill_filters(weight_ref, cols_ref, filt_rows)
    for tile in range(spread.shape[0]):
        spread[tile, : G * GROUP, :] = (
            grad_ref[:, :, tile * LANES : (tile + 1) * LANES]
            .astype(jnp.float32)
            .reshape(G * GROUP, LANES)
        )

    @pl.loop(0, GROUP // SUB)
    def _(batch):
        first = batch * SUB
        filters = [
            filters_of(filt_rows, first + c).T[:SAMPLES_PAD].astype(bf16) for c in range(SUB)
        ]
        filt_grid = dot(jnp.concatenate(filters, axis=0), rad_twice[...])
        sides = []
        for pair in range(0, SUB, 2):
            grads = [
                jnp.concatenate(
                    [
                        spread[tile, pl.ds(first + c, G_PAD, stride=GROUP), :].astype(bf16)
                        for tile in range(spread.shape[0])
                    ],
                    axis=1,
                )
                for c in (pair, pair + 1)
            ]
            both = dot(pair_ref[...], jnp.concatenate(grads, axis=0))
            for c in (pair, pair + 1):
                weighted = both[(c - pair) * SAMPLES_PAD : (c - pair + 1) * SAMPLES_PAD]
                grid_ref[first + c] = weighted.astype(bf16)
                sides.append(
                    (weighted * filt_grid[c * SAMPLES_PAD : (c + 1) * SAMPLES_PAD]).astype(bf16)
                )
        summed = dot(jnp.concatenate(sides, axis=0), sel_t[...]).astype(bf16)
        placed = dot(
            table_ref[...],
            jnp.concatenate(
                [summed[c * SAMPLES_PAD : (c + 1) * SAMPLES_PAD] for c in range(SUB)], axis=1
            ),
        ) * (1.0 / SAMPLES)
        for c in range(SUB):
            turned = placed[:, c * LANES : (c + 1) * LANES].T[:, :G]
            blocks = [
                turned[index * block_len : (index + 1) * block_len]
                for index in range(2 * REACH + 1)
            ]
            own_ref[first + c] = blocks.pop(REACH)
            for sent_ref, block in zip(sent_refs, blocks):
                sent_ref[first + c] = block.astype(bf16)


def filter_kernel(
    grid_ref, weight_ref, code_ref, rad_ref, table_t_ref, rows_ref, cols_ref, *refs
):
    bf16 = jnp.bfloat16
    window_refs, (radial_ref, out_ref, filt_rows, sel, rad_t) = refs[:-5], refs[-5:]
    basis_count = radial_ref.shape[0]

    @pl.when(pl.program_id(0) == 0)
    def _():
        radial_ref[...] = jnp.zeros_like(radial_ref)
        sel[...] = selector(code_ref).astype(bf16)
        rad_t[...] = masked_radial(code_ref, rad_ref).T.astype(bf16)

    fill_filters(weight_ref, cols_ref, filt_rows)
    block_len = window_refs[0].shape[1]
    rest = jnp.zeros((LANES - len(window_refs) * block_len, G), bf16)

    @pl.loop(0, GROUP // SUB)
    def _(batch):
        first = batch * SUB
        windows = []
        for c in range(SUB):
            windows += [ref[first + c] for ref in window_refs] + [rest]
        atom_grid = dot(rows_ref[...], jnp.concatenate(windows, axis=0), ((1,), (1,)))
        atom_grid = (atom_grid[:SAMPLES_PAD] + atom_grid[SAMPLES_PAD:]).astype(bf16)
        feat_grid = dot(
            jnp.concatenate(
                [atom_grid[:, c * LANES : (c + 1) * LANES] for c in range(SUB)], axis=0
            ),
            sel[...],
        )
        sides = jnp.concatenate(
            [
                (
                    grid_ref[first + c].astype(jnp.float32)
                    * feat_grid[c * SAMPLES_PAD : (c + 1) * SAMPLES_PAD]
                ).astype(bf16)
                for c in range(SUB)
            ],
            axis=0,
        )
        summed = dot(sides, rad_t[...])
        turned = jnp.concatenate(
            [summed[c * SAMPLES_PAD : (c + 1) * SAMPLES_PAD].T for c in range(SUB)], axis=0
        )
        coarse = turned.astype(bf16)
        fine = (turned - coarse.astype(jnp.float32)).astype(bf16)
        span = SUB * basis_count
        placed = dot(jnp.concatenate([coarse, fine], axis=0), table_t_ref[0])
        placed = placed[:span] + placed[span:] + dot(coarse, table_t_ref[1])
        out_ref[pl.ds(pl.multiple_of(batch * span, span), span), :] = placed[:, :G].astype(bf16)
        filters = jnp.concatenate(
            [filters_of(filt_rows, first + c)[:, :SAMPLES_PAD] for c in range(SUB)], axis=1
        )
        parts = dot(filters.astype(bf16), sides)
        radial_ref[...] += parts[:basis_count] + parts[basis_count:]


def whole(x):
    return pl.BlockSpec(x.shape, lambda i: (0,) * x.ndim)


def grouped(shape):
    return pl.BlockSpec((GROUP,) + tuple(shape), lambda i: (i, 0, 0))


def grid_call(
    kernel, name, chan_count, out_shape, out_specs, split, special, shared, split_last=(), scratch=()
):
    return pl.pallas_call(
        kernel,
        grid=(chan_count // GROUP,),
        in_specs=[grouped(x.shape[1:]) for x in split]
        + [spec for _, spec in special]
        + [whole(x) for x in shared]
        + [grouped(x.shape[1:]) for x in split_last],
        out_specs=out_specs,
        out_shape=out_shape,
        scratch_shapes=list(scratch),
        compiler_params=pltpu.CompilerParams(vmem_limit_bytes=54 * 1024 * 1024),
        cost_estimate=pl.CostEstimate(
            flops=chan_count * 160_000_000, bytes_accessed=16_000_000, transcendentals=0
        ),
        name=name,
    )(*split, *[x for x, _ in special], *shared, *split_last)


def sum_kernel(
    weight_ref, radial_ref, weight_out, radial_out, parts, slots, send1, recv1, send2, recv2, send3, recv3, own
):
    atoms, reps, chans = (lax.axis_size(name) for name in ("atom", "rep", "chan"))
    atom, rep, chan = (lax.axis_index(name) for name in ("atom", "rep", "chan"))
    count = atoms * reps
    me = atom * reps + rep

    def member(step):
        index = lax.rem(me + step, count)
        return index, {"atom": index // reps, "chan": chan, "rep": lax.rem(index, reps)}

    def other(step):
        return {"atom": atom, "chan": lax.rem(chan + step, chans), "rep": rep}

    own_chunk = pltpu.make_async_copy(weight_ref.at[me], parts.at[0], own.at[0])
    own_radial = pltpu.make_async_copy(radial_ref, slots.at[chan], own.at[1])
    own_chunk.start()
    own_radial.start()
    barrier = pltpu.get_barrier_semaphore()

    @pl.loop(1, count)
    def _(step):
        pl.semaphore_signal(
            barrier, inc=1, device_id=member(step)[1], device_id_type=pl.DeviceIdType.MESH
        )

    for step in range(1, chans):
        pl.semaphore_signal(
            barrier, inc=1, device_id=other(step), device_id_type=pl.DeviceIdType.MESH
        )
    pl.semaphore_wait(barrier, count - 1 + chans - 1)

    def chunk_copy(step):
        index, device = member(step)
        return pltpu.make_async_remote_copy(
            src_ref=weight_ref.at[index],
            dst_ref=parts.at[step],
            send_sem=send1.at[step],
            recv_sem=recv1.at[step],
            device_id=device,
            device_id_type=pl.DeviceIdType.MESH,
        )

    def radial_copy(step):
        return pltpu.make_async_remote_copy(
            src_ref=radial_ref,
            dst_ref=slots.at[chan],
            send_sem=send2.at[step],
            recv_sem=recv2.at[step],
            device_id=other(step),
            device_id_type=pl.DeviceIdType.MESH,
        )

    def total_copy(step):
        return pltpu.make_async_remote_copy(
            src_ref=weight_out.at[me],
            dst_ref=weight_out.at[me],
            send_sem=send3.at[step],
            recv_sem=recv3.at[step],
            device_id=member(step)[1],
            device_id_type=pl.DeviceIdType.MESH,
        )

    @pl.loop(1, count)
    def _(step):
        chunk_copy(step).start()

    for step in range(1, chans):
        radial_copy(step).start()

    @pl.loop(1, count)
    def _(step):
        chunk_copy(step).wait_recv()

    own_chunk.wait()
    total = parts[0].astype(jnp.float32)
    for step in range(1, count):
        total = total + parts[step].astype(jnp.float32)
    weight_out[me] = total.astype(weight_out.dtype)

    @pl.loop(1, count)
    def _(step):
        total_copy(step).start()

    for step in range(1, chans):
        radial_copy(step).wait()
    own_radial.wait()
    radial_total = slots[0]
    for index in range(1, chans):
        radial_total = radial_total + slots[index]
    radial_out[...] = radial_total * (1.0 / SAMPLES)

    @pl.loop(1, count)
    def _(step):
        chunk_copy(step).wait_send()
        total_copy(step).wait()


def sum_call(weight, radial):
    chans = lax.axis_size("chan")
    count = weight.shape[0]
    vmem = pl.BlockSpec(memory_space=pltpu.VMEM)
    anywhere = pl.BlockSpec(memory_space=pl.ANY)
    sizes = (count, count, chans, chans, count, count, 2)
    sems = [pltpu.SemaphoreType.DMA((size,)) for size in sizes]
    return pl.pallas_call(
        sum_kernel,
        in_specs=[anywhere, anywhere],
        out_specs=[vmem, vmem],
        out_shape=[
            jax.ShapeDtypeStruct(weight.shape, weight.dtype),
            jax.ShapeDtypeStruct(radial.shape, jnp.float32),
        ],
        scratch_shapes=[
            pltpu.VMEM(weight.shape, weight.dtype),
            pltpu.VMEM((chans,) + radial.shape, jnp.float32),
        ]
        + sems,
        compiler_params=pltpu.CompilerParams(collective_id=0, has_side_effects=True),
        name="sums",
    )(weight, radial)


def local(feats, neighbors, counts, radial, filter_weight, message_grad):
    exact = basis_table()
    rounded = exact.astype(jnp.bfloat16)
    remainder = (exact - rounded.astype(np.float32)).astype(jnp.bfloat16)
    table = jnp.asarray(rounded)
    table_t = jnp.asarray(np.stack([rounded.T, remainder.T]))
    pair_rows = jnp.asarray(np.kron(np.eye(2, dtype=np.float32), rounded.T.astype(np.float32)), jnp.bfloat16)
    split_rows = jnp.asarray(np.concatenate([rounded[:G].T, remainder[:G].T], axis=0))
    columns = jnp.asarray(np.pad(rounded[:G], ((0, 0), (0, -SAMPLES_PAD % LANES))))
    atom_count = lax.axis_size("atom")
    position = lax.axis_index("atom")
    block_len = feats.shape[3]
    chan_count = feats.shape[1]
    own_block = jnp.transpose(feats[0], (0, 2, 1))
    offsets = [offset for offset in range(-REACH, REACH + 1)]
    window = [
        own_block if offset == 0 else passed_along(own_block, "atom", -offset)
        for offset in offsets
    ]
    sources = neighbors[0].reshape(-1)
    slot_index = (
        sources // block_len - position + REACH
    ) % atom_count * block_len + sources % block_len
    valid = (jnp.arange(SLOTS, dtype=jnp.int32)[None, :] < counts[0][:, None]).reshape(-1)
    code = jnp.where(valid, slot_index, -1)[None, :]
    radial_e = radial[0]
    basis_count = radial_e.shape[0]
    edges = radial_e.shape[1]
    block_shape = (chan_count, block_len, G)
    weight_spec = pl.BlockSpec((basis_count, GROUP, G), lambda i: (0, i, 0))
    filter_scratch = pltpu.VMEM(
        (-(-SAMPLES_PAD // LANES), basis_count * GROUP, LANES), jnp.float32
    )
    grid, own_grad, *outgoing = grid_call(
        feature_kernel,
        "feature_path",
        chan_count,
        [
            jax.ShapeDtypeStruct((chan_count, SAMPLES_PAD, edges), jnp.bfloat16),
            jax.ShapeDtypeStruct(block_shape, jnp.float32),
        ]
        + [jax.ShapeDtypeStruct(block_shape, jnp.bfloat16)] * (2 * REACH),
        [grouped((SAMPLES_PAD, edges))] + [grouped(block_shape[1:])] * (2 * REACH + 1),
        [],
        [
            (filter_weight, weight_spec),
            (
                jnp.transpose(message_grad[0], (1, 0, 2)),
                pl.BlockSpec((G, GROUP, edges), lambda i: (0, i, 0)),
            )
        ],
        [code, radial_e, table, pair_rows, columns],
        scratch=[
            pltpu.VMEM((edges // LANES, G_PAD * GROUP, LANES), jnp.float32),
            filter_scratch,
            pltpu.VMEM((edges, LANES), jnp.bfloat16),
            pltpu.VMEM((2 * basis_count, edges), jnp.bfloat16),
        ],
    )
    arrived = [
        passed_along(block, "atom", offset)
        for offset, block in zip([o for o in offsets if o != 0], outgoing)
    ]
    radial_local, weight_local = grid_call(
        filter_kernel,
        "filter_path",
        chan_count,
        [
            jax.ShapeDtypeStruct((basis_count, edges), jnp.float32),
            jax.ShapeDtypeStruct((chan_count * basis_count, G), jnp.bfloat16),
        ],
        [
            pl.BlockSpec((basis_count, edges), lambda i: (0, 0)),
            pl.BlockSpec((GROUP * basis_count, G), lambda i: (i, 0)),
        ],
        [grid],
        [(filter_weight, weight_spec)],
        [code, radial_e, table_t, split_rows, columns],
        window,
        scratch=[
            filter_scratch,
            pltpu.VMEM((LANES, edges), jnp.bfloat16),
            pltpu.VMEM((edges, basis_count), jnp.bfloat16),
        ],
    )
    sharers = atom_count * lax.axis_size("rep")
    weight_summed, radial_grad = sum_call(weight_local.reshape(sharers, -1, G), radial_local)
    weight_summed = jnp.transpose(weight_summed.reshape(chan_count, basis_count, G), (1, 0, 2))
    weight_grad = weight_summed.astype(jnp.float32) * (1.0 / (SAMPLES * sharers * block_len))
    returned_sum = own_grad
    for block in arrived:
        returned_sum = returned_sum + block.astype(jnp.float32)
    feat_grad = jnp.transpose(returned_sum, (0, 2, 1))[None]
    return (feat_grad, radial_grad[None], weight_grad)


def solution(mesh):
    placed = (
        P("rep", "chan", None, "atom"),
        P("rep", "atom", None),
        P("rep", "atom"),
        P("rep", None, "atom"),
        P(None, "chan", None),
        P("rep", "chan", None, "atom"),
    )
    return jax.shard_map(
        local,
        mesh=mesh,
        in_specs=placed,
        out_specs=(P("rep", "chan", None, "atom"), P("rep", None, "atom"), P(None, "chan", None)),
        check_vma=False,
    )
```

```python
import functools

import jax
import jax.numpy as jnp
import numpy as np
from jax import lax
from jax.experimental import pallas as pl
from jax.experimental.pallas import tpu as pltpu
from jax.sharding import PartitionSpec as P

BASIS = 9
POINTS = 13
SAMPLES = POINTS * POINTS
SAMPLES_PAD = -(-SAMPLES // 16) * 16
SLOTS = 32
REACH = 2
G = 81
G_PAD = 96
GROUP = 16
SUB = 16
LANES = 128


def basis_table():
    points = np.arange(POINTS) * (2.0 * np.pi / POINTS)
    degree_index = np.arange(BASIS)
    angles = ((degree_index + 1) // 2)[:, None] * points[None, :]
    single = np.where(
        degree_index[:, None] == 0,
        1.0,
        np.sqrt(2.0) * np.where(degree_index[:, None] % 2 == 1, np.cos(angles), np.sin(angles)),
    )
    product = (single[:, None, :, None] * single[None, :, None, :]).reshape(G, SAMPLES)
    padded = np.zeros((G_PAD, SAMPLES_PAD), np.float32)
    padded[:G, :SAMPLES] = product
    return padded


def passed_along(value, axis, steps):
    count = lax.axis_size(axis)
    pairs = [(source, (source + steps) % count) for source in range(count)]
    return lax.ppermute(value, axis, pairs)


def dot(a, b, contract=((1,), (0,))):
    return lax.dot_general(a, b, (contract, ((), ())), preferred_element_type=jnp.float32)


def fill_filters(weight_ref, cols_ref, filt_rows):
    basis_count, group, coefficients = weight_ref.shape
    rows = dot(weight_ref[...].reshape(basis_count * group, coefficients), cols_ref[...])
    for half in range(filt_rows.shape[0]):
        filt_rows[half] = rows[:, half * LANES : (half + 1) * LANES]


def filters_of(filt_rows, channel):
    halves = [
        filt_rows[half, pl.ds(channel, filt_rows.shape[1] // GROUP, stride=GROUP), :]
        for half in range(filt_rows.shape[0])
    ]
    value = jnp.concatenate(halves, axis=1)
    coarse = value.astype(jnp.bfloat16).astype(jnp.float32)
    return jnp.concatenate([coarse, value - coarse], axis=0)


def selector(code_ref):
    code = code_ref[...]
    place = lax.broadcasted_iota(jnp.int32, (LANES, code.shape[1]), 0)
    return jnp.where(place == code, 1.0, 0.0)


def masked_radial(code_ref, rad_ref):
    return jnp.where(code_ref[...] >= 0, rad_ref[...].astype(jnp.float32), 0.0)


def feature_kernel(
    weight_ref, grad_ref, code_ref, rad_ref, table_ref, pair_ref, cols_ref, grid_ref, own_ref, *refs
):
    bf16 = jnp.bfloat16
    sent_refs, (spread, filt_rows, sel_t, rad_twice) = refs[:-4], refs[-4:]
    block_len = own_ref.shape[1]

    @pl.when(pl.program_id(0) == 0)
    def _():
        sel_t[...] = selector(code_ref).T.astype(bf16)
        rad = masked_radial(code_ref, rad_ref)
        rad_twice[...] = jnp.concatenate([rad, rad], axis=0).astype(bf16)
        spread[:, G * GROUP :, :] = jnp.zeros(
            (spread.shape[0], (G_PAD - G) * GROUP, LANES), jnp.float32
        )

    fill_filters(weight_ref, cols_ref, filt_rows)
    for tile in range(spread.shape[0]):
        spread[tile, : G * GROUP, :] = (
            grad_ref[:, :, tile * LANES : (tile + 1) * LANES]
            .astype(jnp.float32)
            .reshape(G * GROUP, LANES)
        )

    @pl.loop(0, GROUP // SUB)
    def _(batch):
        first = batch * SUB
        filters = [
            filters_of(filt_rows, first + c).T[:SAMPLES_PAD].astype(bf16) for c in range(SUB)
        ]
        filt_grid = dot(jnp.concatenate(filters, axis=0), rad_twice[...])
        sides = []
        for pair in range(0, SUB, 2):
            grads = [
                jnp.concatenate(
                    [
                        spread[tile, pl.ds(first + c, G_PAD, stride=GROUP), :].astype(bf16)
                        for tile in range(spread.shape[0])
                    ],
                    axis=1,
                )
                for c in (pair, pair + 1)
            ]
            both = dot(pair_ref[...], jnp.concatenate(grads, axis=0))
            for c in (pair, pair + 1):
                weighted = both[(c - pair) * SAMPLES_PAD : (c - pair + 1) * SAMPLES_PAD]
                grid_ref[first + c] = weighted.astype(bf16)
                sides.append(
                    (weighted * filt_grid[c * SAMPLES_PAD : (c + 1) * SAMPLES_PAD]).astype(bf16)
                )
        summed = dot(jnp.concatenate(sides, axis=0), sel_t[...]).astype(bf16)
        placed = dot(
            table_ref[...],
            jnp.concatenate(
                [summed[c * SAMPLES_PAD : (c + 1) * SAMPLES_PAD] for c in range(SUB)], axis=1
            ),
        ) * (1.0 / SAMPLES)
        for c in range(SUB):
            turned = placed[:, c * LANES : (c + 1) * LANES].T[:, :G]
            blocks = [
                turned[index * block_len : (index + 1) * block_len]
                for index in range(2 * REACH + 1)
            ]
            own_ref[first + c] = blocks.pop(REACH)
            for sent_ref, block in zip(sent_refs, blocks):
                sent_ref[first + c] = block.astype(bf16)


def filter_kernel(
    grid_ref, weight_ref, code_ref, rad_ref, table_t_ref, rows_ref, cols_ref, *refs
):
    bf16 = jnp.bfloat16
    window_refs, (radial_ref, out_ref, filt_rows, sel, rad_t) = refs[:-5], refs[-5:]
    basis_count = radial_ref.shape[0]

    @pl.when(pl.program_id(0) == 0)
    def _():
        radial_ref[...] = jnp.zeros_like(radial_ref)
        sel[...] = selector(code_ref).astype(bf16)
        rad_t[...] = masked_radial(code_ref, rad_ref).T.astype(bf16)

    fill_filters(weight_ref, cols_ref, filt_rows)
    block_len = window_refs[0].shape[1]
    rest = jnp.zeros((LANES - len(window_refs) * block_len, G), bf16)

    @pl.loop(0, GROUP // SUB)
    def _(batch):
        first = batch * SUB
        windows = []
        for c in range(SUB):
            windows += [ref[first + c] for ref in window_refs] + [rest]
        atom_grid = dot(rows_ref[...], jnp.concatenate(windows, axis=0), ((1,), (1,)))
        atom_grid = (atom_grid[:SAMPLES_PAD] + atom_grid[SAMPLES_PAD:]).astype(bf16)
        feat_grid = dot(
            jnp.concatenate(
                [atom_grid[:, c * LANES : (c + 1) * LANES] for c in range(SUB)], axis=0
            ),
            sel[...],
        )
        sides = jnp.concatenate(
            [
                (
                    grid_ref[first + c].astype(jnp.float32)
                    * feat_grid[c * SAMPLES_PAD : (c + 1) * SAMPLES_PAD]
                ).astype(bf16)
                for c in range(SUB)
            ],
            axis=0,
        )
        summed = dot(sides, rad_t[...])
        turned = jnp.concatenate(
            [summed[c * SAMPLES_PAD : (c + 1) * SAMPLES_PAD].T for c in range(SUB)], axis=0
        )
        coarse = turned.astype(bf16)
        fine = (turned - coarse.astype(jnp.float32)).astype(bf16)
        span = SUB * basis_count
        placed = dot(jnp.concatenate([coarse, fine], axis=0), table_t_ref[0])
        placed = placed[:span] + placed[span:] + dot(coarse, table_t_ref[1])
        out_ref[pl.ds(pl.multiple_of(batch * span, span), span), :] = placed[:, :G].astype(bf16)
        filters = jnp.concatenate(
            [filters_of(filt_rows, first + c)[:, :SAMPLES_PAD] for c in range(SUB)], axis=1
        )
        parts = dot(filters.astype(bf16), sides)
        radial_ref[...] += parts[:basis_count] + parts[basis_count:]


def whole(x):
    return pl.BlockSpec(x.shape, lambda i: (0,) * x.ndim)


def grouped(shape):
    return pl.BlockSpec((GROUP,) + tuple(shape), lambda i: (i, 0, 0))


def grid_call(
    kernel, name, chan_count, out_shape, out_specs, split, special, shared, split_last=(), scratch=()
):
    return pl.pallas_call(
        kernel,
        grid=(chan_count // GROUP,),
        in_specs=[grouped(x.shape[1:]) for x in split]
        + [spec for _, spec in special]
        + [whole(x) for x in shared]
        + [grouped(x.shape[1:]) for x in split_last],
        out_specs=out_specs,
        out_shape=out_shape,
        scratch_shapes=list(scratch),
        compiler_params=pltpu.CompilerParams(vmem_limit_bytes=54 * 1024 * 1024),
        cost_estimate=pl.CostEstimate(
            flops=chan_count * 160_000_000, bytes_accessed=16_000_000, transcendentals=0
        ),
        name=name,
    )(*split, *[x for x, _ in special], *shared, *split_last)


def sum_kernel(
    weight_ref, radial_ref, weight_out, radial_out, parts, slots, send1, recv1, send2, recv2, send3, recv3, own
):
    atoms, reps, chans = (lax.axis_size(name) for name in ("atom", "rep", "chan"))
    atom, rep, chan = (lax.axis_index(name) for name in ("atom", "rep", "chan"))
    count = atoms * reps
    me = atom * reps + rep

    def member(step):
        index = lax.rem(me + step, count)
        return index, {"atom": index // reps, "chan": chan, "rep": lax.rem(index, reps)}

    def other(step):
        return {"atom": atom, "chan": lax.rem(chan + step, chans), "rep": rep}

    own_chunk = pltpu.make_async_copy(weight_ref.at[me], parts.at[0], own.at[0])
    own_radial = pltpu.make_async_copy(radial_ref, slots.at[chan], own.at[1])
    own_chunk.start()
    own_radial.start()
    barrier = pltpu.get_barrier_semaphore()

    @pl.loop(1, count)
    def _(step):
        pl.semaphore_signal(
            barrier, inc=1, device_id=member(step)[1], device_id_type=pl.DeviceIdType.MESH
        )

    for step in range(1, chans):
        pl.semaphore_signal(
            barrier, inc=1, device_id=other(step), device_id_type=pl.DeviceIdType.MESH
        )
    pl.semaphore_wait(barrier, count - 1 + chans - 1)

    def chunk_copy(step):
        index, device = member(step)
        return pltpu.make_async_remote_copy(
            src_ref=weight_ref.at[index],
            dst_ref=parts.at[step],
            send_sem=send1.at[step],
            recv_sem=recv1.at[step],
            device_id=device,
            device_id_type=pl.DeviceIdType.MESH,
        )

    def radial_copy(step):
        return pltpu.make_async_remote_copy(
            src_ref=radial_ref,
            dst_ref=slots.at[chan],
            send_sem=send2.at[step],
            recv_sem=recv2.at[step],
            device_id=other(step),
            device_id_type=pl.DeviceIdType.MESH,
        )

    def total_copy(step):
        return pltpu.make_async_remote_copy(
            src_ref=weight_out.at[me],
            dst_ref=weight_out.at[me],
            send_sem=send3.at[step],
            recv_sem=recv3.at[step],
            device_id=member(step)[1],
            device_id_type=pl.DeviceIdType.MESH,
        )

    @pl.loop(1, count)
    def _(step):
        chunk_copy(step).start()

    for step in range(1, chans):
        radial_copy(step).start()

    @pl.loop(1, count)
    def _(step):
        chunk_copy(step).wait_recv()

    own_chunk.wait()
    total = parts[0].astype(jnp.float32)
    for step in range(1, count):
        total = total + parts[step].astype(jnp.float32)
    weight_out[me] = total.astype(weight_out.dtype)

    @pl.loop(1, count)
    def _(step):
        total_copy(step).start()

    for step in range(1, chans):
        radial_copy(step).wait()
    own_radial.wait()
    radial_total = slots[0]
    for index in range(1, chans):
        radial_total = radial_total + slots[index]
    radial_out[...] = radial_total

    @pl.loop(1, count)
    def _(step):
        chunk_copy(step).wait_send()
        total_copy(step).wait()


def sum_call(weight, radial):
    chans = lax.axis_size("chan")
    count = weight.shape[0]
    vmem = pl.BlockSpec(memory_space=pltpu.VMEM)
    anywhere = pl.BlockSpec(memory_space=pl.ANY)
    sizes = (count, count, chans, chans, count, count, 2)
    sems = [pltpu.SemaphoreType.DMA((size,)) for size in sizes]
    return pl.pallas_call(
        sum_kernel,
        in_specs=[anywhere, anywhere],
        out_specs=[vmem, vmem],
        out_shape=[
            jax.ShapeDtypeStruct(weight.shape, weight.dtype),
            jax.ShapeDtypeStruct(radial.shape, jnp.float32),
        ],
        scratch_shapes=[
            pltpu.VMEM(weight.shape, weight.dtype),
            pltpu.VMEM((chans,) + radial.shape, jnp.float32),
        ]
        + sems,
        compiler_params=pltpu.CompilerParams(collective_id=0, has_side_effects=True),
        name="sums",
    )(weight, radial)


def local(feats, neighbors, counts, radial, filter_weight, message_grad):
    exact = basis_table()
    rounded = exact.astype(jnp.bfloat16)
    remainder = (exact - rounded.astype(np.float32)).astype(jnp.bfloat16)
    table = jnp.asarray(rounded)
    table_t = jnp.asarray(np.stack([rounded.T, remainder.T]))
    pair_rows = jnp.asarray(np.kron(np.eye(2, dtype=np.float32), rounded.T.astype(np.float32)), jnp.bfloat16)
    split_rows = jnp.asarray(np.concatenate([rounded[:G].T, remainder[:G].T], axis=0))
    columns = jnp.asarray(np.pad(rounded[:G], ((0, 0), (0, -SAMPLES_PAD % LANES))))
    atom_count = lax.axis_size("atom")
    position = lax.axis_index("atom")
    block_len = feats.shape[3]
    chan_count = feats.shape[1]
    own_block = jnp.transpose(feats[0], (0, 2, 1))
    offsets = [offset for offset in range(-REACH, REACH + 1)]
    window = [
        own_block if offset == 0 else passed_along(own_block, "atom", -offset)
        for offset in offsets
    ]
    sources = neighbors[0]
    slot_index = (
        sources // block_len - position + REACH
    ) % atom_count * block_len + sources % block_len
    valid = (jnp.arange(SLOTS, dtype=jnp.int32)[None, :] < counts[0][:, None])
    code = jnp.where(valid, slot_index, -1).reshape(1, -1)
    radial_e = radial[0]
    basis_count = radial_e.shape[0]
    edges = radial_e.shape[1]
    block_shape = (chan_count, block_len, G)
    weight_spec = pl.BlockSpec((basis_count, GROUP, G), lambda i: (0, i, 0))
    filter_scratch = pltpu.VMEM(
        (-(-SAMPLES_PAD // LANES), basis_count * GROUP, LANES), jnp.float32
    )
    grid, own_grad, *outgoing = grid_call(
        feature_kernel,
        "feature_path",
        chan_count,
        [
            jax.ShapeDtypeStruct((chan_count, SAMPLES_PAD, edges), jnp.bfloat16),
            jax.ShapeDtypeStruct(block_shape, jnp.float32),
        ]
        + [jax.ShapeDtypeStruct(block_shape, jnp.bfloat16)] * (2 * REACH),
        [grouped((SAMPLES_PAD, edges))] + [grouped(block_shape[1:])] * (2 * REACH + 1),
        [],
        [
            (filter_weight, weight_spec),
            (
                jnp.transpose(message_grad[0], (1, 0, 2)),
                pl.BlockSpec((G, GROUP, edges), lambda i: (0, i, 0)),
            )
        ],
        [code, radial_e, table, pair_rows, columns],
        scratch=[
            pltpu.VMEM((edges // LANES, G_PAD * GROUP, LANES), jnp.float32),
            filter_scratch,
            pltpu.VMEM((edges, LANES), jnp.bfloat16),
            pltpu.VMEM((2 * basis_count, edges), jnp.bfloat16),
        ],
    )
    arrived = [
        passed_along(block, "atom", offset)
        for offset, block in zip([o for o in offsets if o != 0], outgoing)
    ]
    radial_local, weight_local = grid_call(
        filter_kernel,
        "filter_path",
        chan_count,
        [
            jax.ShapeDtypeStruct((basis_count, edges), jnp.float32),
            jax.ShapeDtypeStruct((chan_count * basis_count, G), jnp.bfloat16),
        ],
        [
            pl.BlockSpec((basis_count, edges), lambda i: (0, 0)),
            pl.BlockSpec((GROUP * basis_count, G), lambda i: (i, 0)),
        ],
        [grid],
        [(filter_weight, weight_spec)],
        [code, radial_e, table_t, split_rows, columns],
        window,
        scratch=[
            filter_scratch,
            pltpu.VMEM((LANES, edges), jnp.bfloat16),
            pltpu.VMEM((edges, basis_count), jnp.bfloat16),
        ],
    )
    sharers = atom_count * lax.axis_size("rep")
    weight_summed, radial_grad = sum_call(weight_local.reshape(sharers, -1, G), radial_local)
    weight_summed = jnp.transpose(weight_summed.reshape(chan_count, basis_count, G), (1, 0, 2))
    weight_grad = weight_summed.astype(jnp.float32) * (1.0 / (SAMPLES * sharers * block_len))
    returned_sum = own_grad
    for block in arrived:
        returned_sum = returned_sum + block.astype(jnp.float32)
    feat_grad = jnp.transpose(returned_sum, (0, 2, 1))[None]
    return (feat_grad, radial_grad[None] * (1.0 / SAMPLES), weight_grad)


def solution(mesh):
    placed = (
        P("rep", "chan", None, "atom"),
        P("rep", "atom", None),
        P("rep", "atom"),
        P("rep", None, "atom"),
        P(None, "chan", None),
        P("rep", "chan", None, "atom"),
    )
    return jax.shard_map(
        local,
        mesh=mesh,
        in_specs=placed,
        out_specs=(P("rep", "chan", None, "atom"), P("rep", None, "atom"), P(None, "chan", None)),
        check_vma=False,
    )
```
